512 devices in a mesh: row: 32 (over y, z_hi, core), col: 16 (over z_lo, x).
Axes of the slice: x: 4, y: 4, z: 16 (z_hi: 4, z_lo: 4; z = z_hi * 4 + z_lo), core: 2. Of those that a mesh axis runs over, the one named last changes fastest.
Arguments:
- alignment: float32 [768, 64, 64], P('row', 'col'), may hold values from -6 to 6
- pair_state: float32 [768, 768, 128], P('row', 'col'), may hold values from -6 to 6
- pair_weights: float32 [8, 768, 768], P(None, 'row', 'col'), may hold values from 0 to 1, as said below
- align_gain: float32 [64], replicated, may hold values from 0.5 to 2
- value_weight: float32 [64, 256], replicated, may hold values from -0.75 to 0.75
- gate_weight: float32 [64, 256], replicated, may hold values from -0.75 to 0.75
- output_weight: float32 [256, 64], replicated, may hold values from -0.375 to 0.375
- outer_gain: float32 [64], replicated, may hold values from 0.5 to 2
- left_weight: float32 [64, 32], replicated, may hold values from -0.75 to 0.75
- right_weight: float32 [64, 32], replicated, may hold values from -0.75 to 0.75
- outer_weight: float32 [1024, 128], replicated, may hold values from -0.75 to 0.75
- outer_bias: float32 [128], replicated, may hold values from -3 to 3
Outputs:
- alignment_out: float32 [768, 64, 64], P('row', 'col')
- pair_out: float32 [768, 768, 128], P('row', 'col')
The draws below stay inside these ranges and needn't reach their ends.
Inputs may be any that keep to these rules, and one draw needn't show every extreme that they name: `pair_weights`: every entry is positive, and for each head and row token the weights over the 768 column tokens sum to one.
All inputs are finite; a program needn't handle non-finite values.
Results may differ from the reference program's by a relative error of at most 0.00011.
Values sent between devices are 32-bit elements; how exact they have to be, the bound alone decides.
No kernel may reach another device: no remote copies, remote signals or barrier semaphores. Data moves between devices by JAX's collectives and lax.ppermute only.
A program may use at most 64 MiB of HBM per device.

```python
import math
import jax
import jax.numpy as jnp
from jax import lax

CM = 64
CZ = 128
HEADS = 8
HEAD_DIM = 32
OUTER = 32
ROWS_DEV = 24
TOKENS = 768
SEQS = 64


def draw_pair_weights(key, part):
    logit_key = jax.random.fold_in(jax.random.fold_in(key, 17), 0)
    logits = 3.0 * jax.random.normal(logit_key, (HEADS, TOKENS, TOKENS), jnp.float32)
    return jax.nn.softmax(logits, axis=-1)


def level_of(key, extent, shards, low, high):
    loudness, own = 1.0, jax.random.fold_in(key, 6)
    for position, parts in shards:
        heights = jnp.exp(jax.random.uniform(jax.random.fold_in(own, position), (parts,), jnp.float32, low / len(shards), high / len(shards)))
        loudness = loudness * jnp.repeat(heights, extent[position] // parts).reshape([-1 if axis == position else 1 for axis in range(len(extent))])
    return loudness


def gaussian(stream_key, shape, scale, reach, pieces=(), held_as=jnp.bfloat16):
    entries = jax.random.normal(stream_key, shape, jnp.float32) * scale
    if len(pieces) > 0:
        entries = level_of(stream_key, shape, pieces, -0.22, 0.18) * entries
    return jnp.clip(entries, min=-reach, max=reach).astype(held_as)


def setup_inputs(seed: int = 0) -> dict:
    arg_keys = jax.random.split(jax.random.key(seed), 13)
    return {
        "alignment": gaussian(arg_keys[0], (TOKENS, SEQS, CM), 1.0, 6.0, ((0, 32), (1, 16)), jnp.float32),
        "pair_state": gaussian(arg_keys[1], (TOKENS, TOKENS, CZ), 1.0, 6.0, ((0, 32), (1, 16)), jnp.float32),
        "pair_weights": draw_pair_weights(jax.random.fold_in(arg_keys[12], 71), 0),
        "align_gain": jnp.clip(jnp.exp(jax.random.uniform(arg_keys[3], (CM,), jnp.float32, math.log(0.5), math.log(2.0))), 0.5, 2.0),
        "value_weight": gaussian(arg_keys[4], (CM, HEADS * HEAD_DIM), CM ** -0.5, 0.75, (), jnp.float32),
        "gate_weight": gaussian(arg_keys[5], (CM, HEADS * HEAD_DIM), CM ** -0.5, 0.75, (), jnp.float32),
        "output_weight": gaussian(arg_keys[6], (HEADS * HEAD_DIM, CM), (HEADS * HEAD_DIM) ** -0.5, 0.375, (), jnp.float32),
        "outer_gain": jnp.clip(jnp.exp(jax.random.uniform(arg_keys[7], (CM,), jnp.float32, math.log(0.5), math.log(2.0))), 0.5, 2.0),
        "left_weight": gaussian(arg_keys[8], (CM, OUTER), CM ** -0.5, 0.75, (), jnp.float32),
        "right_weight": gaussian(arg_keys[9], (CM, OUTER), CM ** -0.5, 0.75, (), jnp.float32),
        "outer_weight": gaussian(arg_keys[10], (OUTER * OUTER, CZ), (max(OUTER * OUTER // 16, 1)) ** -0.5, 0.75, (), jnp.float32),
        "outer_bias": gaussian(arg_keys[11], (CZ,), 0.5, 3.0, (), jnp.float32),
    }


PRECISE = lax.Precision.HIGHEST

def normalize(features, channel_gain):
    channel_mean = lax.optimization_barrier(jnp.mean(features, axis=-1, keepdims=True))
    centered = features - channel_mean
    spread = lax.optimization_barrier(jnp.mean(centered * centered, axis=-1, keepdims=True))
    return centered * lax.rsqrt(spread + 1e-05) * channel_gain

def reference(alignment, pair_state, pair_weights, align_gain, value_weight, gate_weight, output_weight, outer_gain, left_weight, right_weight, outer_weight, outer_bias):
    head_count = pair_weights.shape[0]
    normed = normalize(alignment, align_gain)
    values = jnp.einsum('nsc,cd->nsd', normed, value_weight, precision=PRECISE)
    values = values.reshape(values.shape[0], values.shape[1], head_count, -1)
    averaged = jnp.einsum('hij,jshd->ishd', pair_weights, values, precision=PRECISE)
    gate_values = jax.nn.sigmoid(jnp.einsum('nsc,cd->nsd', normed, gate_weight, precision=PRECISE))
    gated_heads = gate_values * averaged.reshape(gate_values.shape)
    alignment_out = alignment + jnp.einsum('nsd,dc->nsc', gated_heads, output_weight, precision=PRECISE)
    normed_out = normalize(alignment_out, outer_gain)
    left_side = jnp.einsum('nsc,cd->nsd', normed_out, left_weight, precision=PRECISE)
    right_side = jnp.einsum('nsc,cd->nsd', normed_out, right_weight, precision=PRECISE)
    sequences = alignment.shape[1]
    left_blocks = left_side.reshape(-1, ROWS_DEV, sequences, left_side.shape[2])

    def outer_block(left_block):
        product = jnp.einsum('isc,jsd->ijcd', left_block, right_side, precision=PRECISE) / sequences
        flattened = product.reshape(-1, product.shape[2] * product.shape[3])
        projected = jnp.dot(flattened, outer_weight, precision=PRECISE, preferred_element_type=jnp.float32)
        return projected.reshape(left_block.shape[0], right_side.shape[0], -1)
    update = lax.map(outer_block, left_blocks).reshape(pair_state.shape)
    pair_out = pair_state + update + outer_bias
    return (alignment_out, pair_out)
```

```python
import functools

import jax
import jax.numpy as jnp
from jax import lax
from jax.experimental import pallas as pl
from jax.experimental.pallas import tpu as pltpu
from jax.sharding import Mesh, PartitionSpec as P

F32 = jnp.float32
BF16 = jnp.bfloat16
ROW = ("y", "zh", "core")
COL = ("zl", "x")
ALL = ROW + COL
LANES = 128


def split(value):
    high = value.astype(BF16)
    low = (value - high.astype(F32)).astype(BF16)
    return high, low


def dot(a, b):
    return jnp.dot(a, b, preferred_element_type=F32)


def dot3(a, b):
    ah, al = split(a)
    bh, bl = split(b)
    return dot(ah, bh) + (dot(ah, bl) + dot(al, bh))


def normalize(features, gain):
    mean = jnp.mean(features, axis=-1, keepdims=True)
    centered = features - mean
    spread = jnp.mean(centered * centered, axis=-1, keepdims=True)
    return centered * lax.rsqrt(spread + 1e-05) * gain


def twice(weight):
    zeros = jnp.zeros_like(weight)
    return jnp.concatenate(
        [jnp.concatenate([weight, zeros], 1), jnp.concatenate([zeros, weight], 1)], 0
    )


def prepare_kernel(align_ref, pair_w_ref, gain_ref, normed_ref, weights_ref):
    rows = align_ref.shape[0]
    heads, _, columns = pair_w_ref.shape
    parts = [normalize(align_ref[:, s, :], gain_ref[...]) for s in range(4)]
    normed_ref[0:rows, :] = jnp.concatenate(parts[0:2], axis=1)
    normed_ref[rows : 2 * rows, :] = jnp.concatenate(parts[2:4], axis=1)
    turned = pair_w_ref[...].reshape(heads * rows, columns).T
    half = columns // 2
    tail = turned[:, LANES:]
    tail = jnp.concatenate([tail[:half], tail[half:]], axis=1)
    for k in range(weights_ref.shape[0]):
        weights_ref[k, 0:columns, :] = turned[:, :LANES]
        weights_ref[k, columns:, :] = tail


def average_kernel(
    weights_ref,
    gathered_ref,
    normed_ref,
    align_ref,
    value_ref,
    gate_ref,
    output_ref,
    gain_ref,
    sides_ref,
    out_ref,
    left_ref,
    right_ref,
    left_tmp,
    right_tmp,
):
    rows = align_ref.shape[0]
    columns = 2 * rows
    heads = 8
    first = weights_ref[:, 0:columns, :].reshape(-1, LANES)
    tail = weights_ref[:, columns:, :]
    second = jnp.concatenate([tail[:, :, :64], tail[:, :, 64:]], axis=1).reshape(-1, 64)
    weights = jnp.concatenate([first.T, second.T], axis=0)
    value2 = twice(value_ref[...])
    gate2 = twice(gate_ref[...])
    lane = lax.broadcasted_iota(jnp.int32, (rows, 512), 1)
    lane_head = lax.rem(lax.div(lane, 32), heads)
    wh, wl = split(weights)
    vh, vl = split(value2)
    gated = []
    for p in range(2):
        blocks = [
            gathered_ref[(r % 2) * 16 + r // 2, p * rows : (p + 1) * rows, :] for r in range(32)
        ]
        fh, fl = split(jnp.concatenate(blocks, axis=0))
        mixed = dot(wh, fh) + (dot(wh, fl) + dot(wl, fh))
        mh, ml = split(mixed)
        by_head = dot(mh, vh) + (dot(mh, vl) + dot(ml, vh))
        averaged = jnp.zeros((rows, 512), F32)
        for h in range(heads):
            averaged += jnp.where(lane_head == h, by_head[h * rows : (h + 1) * rows], 0.0)
        gate = jax.nn.sigmoid(dot3(normed_ref[p * rows : (p + 1) * rows, :], gate2))
        product = gate * averaged
        gated += [product[:, :256], product[:, 256:]]
    update = dot3(jnp.concatenate(gated, axis=0), output_ref[...])
    aligned = jnp.concatenate([align_ref[:, s, :] for s in range(4)], axis=0) + update
    for s in range(4):
        out_ref[:, s, :] = aligned[s * rows : (s + 1) * rows]
    sides = dot3(normalize(aligned, gain_ref[...]), sides_ref[...])
    left_tmp[...] = sides[:, :LANES]
    right_tmp[...] = sides[:, LANES:]
    left = jnp.concatenate(
        [left_tmp[pl.ds(k, rows, stride=4), 0:32] for k in range(4)], axis=1
    )
    right = jnp.concatenate(
        [right_tmp[pl.ds(k, rows, stride=4), 0:32] for k in range(4)], axis=1
    )
    for k in range(left_ref.shape[0]):
        left_ref[k] = left
    right_ref[...] = right


CHUNK = 4


def outer_kernel(
    left_ref,
    right_ref,
    state_ref,
    outer_ref,
    bias_ref,
    out_ref,
    turned,
    spread_h,
    spread_l,
    total,
):
    lefts = [
        left_ref[pl.ds(g, 64, stride=6), :] * (1.0 / 64.0) for g in range(6)
    ]
    left = jnp.concatenate(lefts, axis=1)
    lh, ll = split(left)
    left4 = jnp.concatenate([lh, lh, ll, ll], axis=0)
    for core in range(2):
        for g in range(6):
            block = right_ref[pl.ds(core * 384 + g, 64, stride=6), :]
            high = block.astype(BF16).astype(F32)
            stacked = jnp.concatenate([high, block - high], axis=0)
            turned[(core * 6 + g) * LANES : (core * 6 + g + 1) * LANES, :] = stacked.T
    spread_h[...] = jnp.zeros_like(spread_h)
    spread_l[...] = jnp.zeros_like(spread_l)
    for t in range(32 // CHUNK):
        rights = []
        for e in range(CHUNK):
            d = t * CHUNK + e
            right = turned[pl.ds(d, 48, stride=32), :].astype(BF16)
            rights.append(jnp.concatenate([right, right], axis=1))
            wh, wl = split(outer_ref[pl.ds(d, 32, stride=32), :])
            for k in range(4):
                at = (pl.ds(e * LANES + 32 * k, 32), pl.ds(k * LANES, LANES))
                spread_h[at] = wh
                spread_l[at] = wl
        product = dot(jnp.concatenate(rights, axis=0), left4)
        ph, pl_ = split(product)

        def regroup(x):
            return jnp.concatenate(
                [
                    jnp.concatenate(
                        [
                            x[e * 48 : (e + 1) * 48, g * LANES : (g + 1) * LANES]
                            for e in range(CHUNK)
                        ],
                        axis=1,
                    )
                    for g in range(6)
                ],
                axis=0,
            )

        ah, al = regroup(ph), regroup(pl_)
        bh, bl = spread_h[...], spread_l[...]
        step = dot(ah, bh) + (dot(ah, bl) + dot(al, bh))
        if t == 0:
            total[...] = step
        else:
            total[...] += step
    for g in range(6):
        for k in range(4):
            out_ref[g * 4 + k] = (
                state_ref[g * 4 + k]
                + total[g * 48 : (g + 1) * 48, k * LANES : (k + 1) * LANES]
                + bias_ref[...]
            )


def copies(value, axis):
    return jnp.broadcast_to(value[None], (lax.axis_size(axis), *value.shape))


def everyone(value, axis):
    return lax.all_to_all(copies(value, axis), axis, 0, 0, tiled=True)


def to_columns():
    pairs = []
    for y in range(4):
        for zh in range(4):
            for core in range(2):
                for zl in range(4):
                    for x in range(4):
                        source = (((y * 4 + zh) * 2 + core) * 4 + zl) * 4 + x
                        target = (((zl * 4 + x) * 2 + core) * 4 + y) * 4 + zh
                        pairs.append((source, target))
    return pairs


PARAMS = pltpu.CompilerParams(vmem_limit_bytes=48 * 1024 * 1024)


def shape(*dims):
    return jax.ShapeDtypeStruct(dims, F32)


def on_device(
    alignment,
    pair_state,
    pair_weights,
    align_gain,
    value_weight,
    gate_weight,
    output_weight,
    outer_gain,
    left_weight,
    right_weight,
    outer_weight,
    outer_bias,
):
    normed, packed = pl.pallas_call(
        prepare_kernel,
        out_shape=(shape(48, 128), shape(16, 72, 128)),
        compiler_params=PARAMS,
    )(alignment, pair_weights, align_gain[None])
    weights = lax.all_to_all(packed, COL, 0, 0, tiled=True)
    near = lax.all_gather(normed, "zh", axis=0, tiled=True)
    wide = everyone(near, "y").reshape(16 * 48, 128)
    gathered = lax.all_gather(wide, "core", axis=0, tiled=True).reshape(32, 48, 128)
    pad = jnp.zeros((64, 96), F32)
    sides = jnp.concatenate([left_weight, pad, right_weight, pad], axis=1)
    alignment_out, left, right = pl.pallas_call(
        average_kernel,
        out_shape=(shape(24, 4, 64), shape(16, 24, 128), shape(24, 128)),
        scratch_shapes=[pltpu.VMEM((96, 128), F32), pltpu.VMEM((96, 128), F32)],
        compiler_params=PARAMS,
    )(
        weights,
        gathered,
        normed,
        alignment,
        value_weight,
        gate_weight,
        output_weight,
        outer_gain[None],
        sides,
    )
    left_all = lax.all_to_all(left, COL, 0, 0, tiled=True).reshape(384, 128)
    right = lax.ppermute(right, ALL, to_columns())
    right = everyone(right, "zh").reshape(96, 128)
    right = everyone(right, "y").reshape(384, 128)
    right_all = lax.all_gather(right, "core", axis=0, tiled=True)
    pair_out = pl.pallas_call(
        outer_kernel,
        out_shape=shape(24, 48, 128),
        scratch_shapes=[
            pltpu.VMEM((1536, 128), F32),
            pltpu.VMEM((CHUNK * LANES, 512), BF16),
            pltpu.VMEM((CHUNK * LANES, 512), BF16),
            pltpu.VMEM((288, 512), F32),
        ],
        compiler_params=PARAMS,
    )(left_all, right_all, pair_state, outer_weight, outer_bias[None])
    return alignment_out, pair_out


def solution(mesh):
    torus = Mesh(mesh.devices.reshape(4, 4, 2, 4, 4), ALL)
    return jax.shard_map(
        on_device,
        mesh=torus,
        in_specs=(P(ROW, COL, None), P(ROW, COL, None), P(None, ROW, COL)) + (P(),) * 9,
        out_specs=(P(ROW, COL, None), P(ROW, COL, None)),
        check_vma=False,
    )
```

```python
import functools

import jax
import jax.numpy as jnp
from jax import lax
from jax.experimental import pallas as pl
from jax.experimental.pallas import tpu as pltpu
from jax.sharding import Mesh, PartitionSpec as P

F32 = jnp.float32
BF16 = jnp.bfloat16
ROW = ("y", "zh", "core")
COL = ("zl", "x")
ALL = ROW + COL
LANES = 128


def split(value):
    high = value.astype(BF16)
    low = (value - high.astype(F32)).astype(BF16)
    return high, low


def dot(a, b):
    return jnp.dot(a, b, preferred_element_type=F32)


def dot3(a, b):
    ah, al = split(a)
    bh, bl = split(b)
    return dot(ah, bh) + (dot(ah, bl) + dot(al, bh))


def normalize(features, gain):
    mean = jnp.mean(features, axis=-1, keepdims=True)
    centered = features - mean
    spread = jnp.mean(centered * centered, axis=-1, keepdims=True)
    return centered * lax.rsqrt(spread + 1e-05) * gain


def twice(weight):
    zeros = jnp.zeros_like(weight)
    return jnp.concatenate(
        [jnp.concatenate([weight, zeros], 1), jnp.concatenate([zeros, weight], 1)], 0
    )


def prepare_kernel(align_ref, pair_w_ref, gain_ref, normed_ref, weights_ref):
    rows = align_ref.shape[0]
    heads, _, columns = pair_w_ref.shape
    parts = [normalize(align_ref[:, s, :], gain_ref[...]) for s in range(4)]
    normed_ref[0:rows, :] = jnp.concatenate(parts[0:2], axis=1)
    normed_ref[rows : 2 * rows, :] = jnp.concatenate(parts[2:4], axis=1)
    turned = pair_w_ref[...].reshape(heads * rows, columns).T
    half = columns // 2
    tail = turned[:, LANES:]
    tail = jnp.concatenate([tail[:half], tail[half:]], axis=1)
    for k in range(weights_ref.shape[0]):
        weights_ref[k, 0:columns, :] = turned[:, :LANES]
        weights_ref[k, columns:, :] = tail


def average_kernel(
    weights_ref,
    gathered_ref,
    normed_ref,
    align_ref,
    value_ref,
    gate_ref,
    output_ref,
    gain_ref,
    sides_ref,
    out_ref,
    left_ref,
    right_ref,
    left_tmp,
    right_tmp,
):
    rows = align_ref.shape[0]
    columns = 2 * rows
    heads = 8
    first = weights_ref[:, 0:columns, :].reshape(-1, LANES)
    tail = weights_ref[:, columns:, :]
    second = jnp.concatenate([tail[:, :, :64], tail[:, :, 64:]], axis=1).reshape(-1, 64)
    weights = jnp.concatenate([first.T, second.T], axis=0)
    value2 = twice(value_ref[...])
    gate2 = twice(gate_ref[...])
    lane = lax.broadcasted_iota(jnp.int32, (rows, 512), 1)
    lane_head = lax.rem(lax.div(lane, 32), heads)
    wh, wl = split(weights)
    vh, vl = split(value2)
    gated = []
    for p in range(2):
        blocks = [
            gathered_ref[(r % 2) * 16 + r // 2, p * rows : (p + 1) * rows, :] for r in range(32)
        ]
        fh, fl = split(jnp.concatenate(blocks, axis=0))
        mixed = dot(wh, fh) + (dot(wh, fl) + dot(wl, fh))
        mh, ml = split(mixed)
        by_head = dot(mh, vh) + (dot(mh, vl) + dot(ml, vh))
        averaged = jnp.zeros((rows, 512), F32)
        for h in range(heads):
            averaged += jnp.where(lane_head == h, by_head[h * rows : (h + 1) * rows], 0.0)
        gate = jax.nn.sigmoid(dot3(normed_ref[p * rows : (p + 1) * rows, :], gate2))
        product = gate * averaged
        gated += [product[:, :256], product[:, 256:]]
    update = dot3(jnp.concatenate(gated, axis=0), output_ref[...])
    aligned = jnp.concatenate([align_ref[:, s, :] for s in range(4)], axis=0) + update
    for s in range(4):
        out_ref[:, s, :] = aligned[s * rows : (s + 1) * rows]
    sides = dot3(normalize(aligned, gain_ref[...]), sides_ref[...])
    left_tmp[...] = sides[:, :LANES]
    right_tmp[...] = sides[:, LANES:]
    left = jnp.concatenate(
        [left_tmp[pl.ds(k, rows, stride=4), 0:32] for k in range(4)], axis=1
    )
    right = jnp.concatenate(
        [right_tmp[pl.ds(k, rows, stride=4), 0:32] for k in range(4)], axis=1
    )
    for k in range(left_ref.shape[0]):
        left_ref[k] = left
    right_ref[...] = right


CHUNK = 4


def outer_kernel(
    left_ref,
    right_ref,
    state_ref,
    outer_ref,
    bias_ref,
    out_ref,
    turned,
    spread_h,
    spread_l,
    total,
):
    lefts = [
        left_ref[pl.ds(g, 64, stride=6), :] * (1.0 / 64.0) for g in range(6)
    ]
    left = jnp.concatenate(lefts, axis=1)
    lh, ll = split(left)
    left4 = jnp.concatenate([lh, lh, ll, ll], axis=0)
    for core in range(2):
        for g in range(6):
            block = right_ref[pl.ds(core * 384 + g, 64, stride=6), :]
            high = block.astype(BF16).astype(F32)
            stacked = jnp.concatenate([high, block - high], axis=0)
            turned[(core * 6 + g) * LANES : (core * 6 + g + 1) * LANES, :] = stacked.T
    spread_h[...] = jnp.zeros_like(spread_h)
    spread_l[...] = jnp.zeros_like(spread_l)
    for t in range(32 // CHUNK):
        rights = []
        for e in range(CHUNK):
            d = t * CHUNK + e
            right = turned[pl.ds(d, 48, stride=32), :].astype(BF16)
            rights.append(jnp.concatenate([right, right], axis=1))
            wh, wl = split(outer_ref[pl.ds(d, 32, stride=32), :])
            for k in range(4):
                at = (pl.ds(e * LANES + 32 * k, 32), pl.ds(k * LANES, LANES))
                spread_h[at] = wh
                spread_l[at] = wl
        product = dot(jnp.concatenate(rights, axis=0), left4)
        ph, pl_ = split(product)

        def regroup(x):
            return jnp.concatenate(
                [
                    jnp.concatenate(
                        [
                            x[e * 48 : (e + 1) * 48, g * LANES : (g + 1) * LANES]
                            for e in range(CHUNK)
                        ],
                        axis=1,
                    )
                    for g in range(6)
                ],
                axis=0,
            )

        ah, al = regroup(ph), regroup(pl_)
        bh, bl = spread_h[...], spread_l[...]
        step = dot(ah, bh) + (dot(ah, bl) + dot(al, bh))
        if t == 0:
            total[...] = step
        else:
            total[...] += step
    for g in range(6):
        for k in range(4):
            out_ref[g * 4 + k] = (
                state_ref[g * 4 + k]
                + total[g * 48 : (g + 1) * 48, k * LANES : (k + 1) * LANES]
                + bias_ref[...]
            )


def copies(value, axis):
    return jnp.broadcast_to(value[None], (lax.axis_size(axis), *value.shape))


def everyone(value, axis):
    return lax.all_to_all(copies(value, axis), axis, 0, 0, tiled=True)


def to_columns():
    pairs = []
    for y in range(4):
        for zh in range(4):
            for core in range(2):
                for zl in range(4):
                    for x in range(4):
                        source = (((y * 4 + zh) * 2 + core) * 4 + zl) * 4 + x
                        target = (((zl * 4 + x) * 2 + core) * 4 + y) * 4 + zh
                        pairs.append((source, target))
    return pairs


PARAMS = pltpu.CompilerParams(vmem_limit_bytes=48 * 1024 * 1024)


def shape(*dims):
    return jax.ShapeDtypeStruct(dims, F32)


def on_device(
    alignment,
    pair_state,
    pair_weights,
    align_gain,
    value_weight,
    gate_weight,
    output_weight,
    outer_gain,
    left_weight,
    right_weight,
    outer_weight,
    outer_bias,
):
    normed, packed = pl.pallas_call(
        prepare_kernel,
        out_shape=(shape(48, 128), shape(16, 72, 128)),
        compiler_params=PARAMS,
    )(alignment, pair_weights, align_gain[None])
    weights = lax.all_to_all(packed, COL, 0, 0, tiled=True)
    near = lax.all_gather(normed, "zh", axis=0, tiled=True)
    near, weights = lax.optimization_barrier((near, weights))
    wide = everyone(near, "y").reshape(16 * 48, 128)
    gathered = lax.all_gather(wide, "core", axis=0, tiled=True).reshape(32, 48, 128)
    pad = jnp.zeros((64, 96), F32)
    sides = jnp.concatenate([left_weight, pad, right_weight, pad], axis=1)
    alignment_out, left, right = pl.pallas_call(
        average_kernel,
        out_shape=(shape(24, 4, 64), shape(16, 24, 128), shape(24, 128)),
        scratch_shapes=[pltpu.VMEM((96, 128), F32), pltpu.VMEM((96, 128), F32)],
        compiler_params=PARAMS,
    )(
        weights,
        gathered,
        normed,
        alignment,
        value_weight,
        gate_weight,
        output_weight,
        outer_gain[None],
        sides,
    )
    left_all = lax.all_to_all(left, COL, 0, 0, tiled=True).reshape(384, 128)
    right = lax.ppermute(right, ALL, to_columns())
    right, left_all = lax.optimization_barrier((right, left_all))
    right = everyone(right, "zh").reshape(96, 128)
    right = everyone(right, "y").reshape(384, 128)
    right_all = lax.all_gather(right, "core", axis=0, tiled=True)
    pair_out = pl.pallas_call(
        outer_kernel,
        out_shape=shape(24, 48, 128),
        scratch_shapes=[
            pltpu.VMEM((1536, 128), F32),
            pltpu.VMEM((CHUNK * LANES, 512), BF16),
            pltpu.VMEM((CHUNK * LANES, 512), BF16),
            pltpu.VMEM((288, 512), F32),
        ],
        compiler_params=PARAMS,
    )(left_all, right_all, pair_state, outer_weight, outer_bias[None])
    return alignment_out, pair_out


def solution(mesh):
    torus = Mesh(mesh.devices.reshape(4, 4, 2, 4, 4), ALL)
    return jax.shard_map(
        on_device,
        mesh=torus,
        in_specs=(P(ROW, COL, None), P(ROW, COL, None), P(None, ROW, COL)) + (P(),) * 9,
        out_specs=(P(ROW, COL, None), P(ROW, COL, None)),
        check_vma=False,
    )
```

```python
import functools

import jax
import jax.numpy as jnp
from jax import lax
from jax.experimental import pallas as pl
from jax.experimental.pallas import tpu as pltpu
from jax.sharding import Mesh, PartitionSpec as P

F32 = jnp.float32
BF16 = jnp.bfloat16
ROW = ("y", "zh", "core")
COL = ("zl", "x")
ALL = ROW + COL
LANES = 128
HALVES = (slice(0, 64), slice(64, 128))


def split(value):
    high = value.astype(BF16)
    low = (value - high.astype(F32)).astype(BF16)
    return high, low


def dot(a, b):
    return jnp.dot(a, b, preferred_element_type=F32)


def dot3(a, b):
    ah, al = split(a)
    bh, bl = split(b)
    return dot(ah, bh) + (dot(ah, bl) + dot(al, bh))


def normalize(features, gain):
    mean = jnp.mean(features, axis=-1, keepdims=True)
    centered = features - mean
    spread = jnp.mean(centered * centered, axis=-1, keepdims=True)
    return centered * lax.rsqrt(spread + 1e-05) * gain


def twice(weight):
    zeros = jnp.zeros_like(weight)
    return jnp.concatenate(
        [jnp.concatenate([weight, zeros], 1), jnp.concatenate([zeros, weight], 1)], 0
    )


def fill(ref, value):
    if len(ref.shape) == 2:
        ref[...] = value
    else:
        for k in range(ref.shape[0]):
            ref[k] = value


def features_kernel(align_ref, gain_ref, normed_ref):
    parts = [normalize(align_ref[:, s, :], gain_ref[...]) for s in range(4)]
    features = jnp.concatenate(
        [jnp.concatenate(parts[0:2], axis=1), jnp.concatenate(parts[2:4], axis=1)], axis=0
    )
    fill(normed_ref, features)


def weights_kernel(pair_w_ref, weights_ref):
    heads, rows, columns = pair_w_ref.shape
    turned = pair_w_ref[...].reshape(heads * rows, columns).T
    half = columns // 2
    tail = turned[:, LANES:]
    tail = jnp.concatenate([tail[:half], tail[half:]], axis=1)
    fill(weights_ref, jnp.concatenate([turned[:, :LANES], tail], axis=0))


def dot3_turned(a, b):
    ah, al = split(a)
    bh, bl = split(b)

    def one(x, y):
        return lax.dot_general(x, y, (((1,), (1,)), ((), ())), preferred_element_type=F32)

    return one(ah, bh) + (one(ah, bl) + one(al, bh))


def landed(row):
    y, zh, core = row // 8, row // 2 % 4, row % 2
    return (y * 2 + core) * 4 + zh


def average_kernel(
    weights_ref,
    gathered_ref,
    align_hbm,
    value_hbm,
    gate_hbm,
    output_hbm,
    left_hbm,
    right_hbm,
    align_gain_hbm,
    outer_gain_hbm,
    out_ref,
    left_ref,
    right_ref,
    align_ref,
    value_ref,
    gate_ref,
    output_ref,
    left_w_ref,
    right_w_ref,
    align_gain_ref,
    outer_gain_ref,
    left_tmp,
    right_tmp,
    arrived,
):
    fetches = [
        pltpu.make_async_copy(source, target, arrived.at[n])
        for n, (source, target) in enumerate(
            [
                (value_hbm, value_ref),
                (align_hbm, align_ref),
                (align_gain_hbm, align_gain_ref),
                (gate_hbm, gate_ref),
                (output_hbm, output_ref),
                (left_hbm, left_w_ref),
                (right_hbm, right_w_ref),
                (outer_gain_hbm, outer_gain_ref),
            ]
        )
    ]
    for fetch in fetches:
        fetch.start()
    rows = align_ref.shape[0]
    columns = 2 * rows
    heads = 8
    first = weights_ref[:, 0:columns, :].reshape(-1, LANES)
    tails = [weights_ref[k, columns:, :] for k in range(16)]
    second = jnp.concatenate([t[:, half] for t in tails for half in HALVES], axis=0)
    weights = jnp.concatenate([first.T, second.T], axis=0)
    wh, wl = split(weights)
    mixed = []
    for p in range(2):
        blocks = [
            gathered_ref[landed(r), p * rows : (p + 1) * rows, :] for r in range(32)
        ]
        fh, fl = split(jnp.concatenate(blocks, axis=0))
        mixed.append(dot(wh, fh) + (dot(wh, fl) + dot(wl, fh)))
    for fetch in fetches:
        fetch.wait()
    lane = lax.broadcasted_iota(jnp.int32, (rows, 512), 1)
    lane_head = lax.rem(lax.div(lane, 32), heads)
    vh, vl = split(twice(value_ref[...]))
    gate2 = twice(gate_ref[...])
    own = [normalize(align_ref[:, s, :], align_gain_ref[...]) for s in range(4)]
    gated = []
    for p in range(2):
        mh, ml = split(mixed[p])
        by_head = dot(mh, vh) + (dot(mh, vl) + dot(ml, vh))
        averaged = jnp.zeros((rows, 512), F32)
        for h in range(heads):
            averaged += jnp.where(lane_head == h, by_head[h * rows : (h + 1) * rows], 0.0)
        gate = jax.nn.sigmoid(dot3(jnp.concatenate(own[2 * p : 2 * p + 2], axis=1), gate2))
        product = gate * averaged
        gated += [product[:, :256], product[:, 256:]]
    update = dot3_turned(jnp.concatenate(gated, axis=0), output_ref[...])
    aligned = jnp.concatenate([align_ref[:, s, :] for s in range(4)], axis=0) + update
    for s in range(4):
        out_ref[:, s, :] = aligned[s * rows : (s + 1) * rows]
    normed = normalize(aligned, outer_gain_ref[...])
    left_tmp[:, 0:32] = dot3_turned(normed, left_w_ref[...])
    right_tmp[:, 0:32] = dot3_turned(normed, right_w_ref[...])
    left = jnp.concatenate(
        [left_tmp[pl.ds(k, rows, stride=4), 0:32] for k in range(4)], axis=1
    )
    right = jnp.concatenate(
        [right_tmp[pl.ds(k, rows, stride=4), 0:32] for k in range(4)], axis=1
    )
    fill(left_ref, left)
    fill(right_ref, right)


CHUNK = 8


def outer_kernel(
    left_ref,
    right_ref,
    state_ref,
    outer_ref,
    bias_hbm,
    out_ref,
    turned,
    spread_h,
    spread_l,
    total,
    bias_ref,
    arrived,
):
    fetch = pltpu.make_async_copy(bias_hbm, bias_ref, arrived)
    fetch.start()
    lefts = [left_ref[pl.ds(g, 64, stride=6), :] * (1.0 / 64.0) for g in range(6)]
    lh, ll = split(jnp.concatenate(lefts, axis=1))
    left4 = jnp.concatenate([lh, lh, ll, ll], axis=0)
    for core in range(2):
        for g in range(6):
            block = right_ref[pl.ds(core * 384 + g, 64, stride=6), :]
            high = block.astype(BF16).astype(F32)
            stacked = jnp.concatenate([high, block - high], axis=0)
            turned[(core * 6 + g) * LANES : (core * 6 + g + 1) * LANES, :] = stacked.T
    spread_h[...] = jnp.zeros_like(spread_h)
    spread_l[...] = jnp.zeros_like(spread_l)
    low_lanes = lax.broadcasted_iota(jnp.int32, (48, LANES), 1) < 64
    for t in range(32 // CHUNK):
        rights = []
        for e in range(CHUNK):
            d = t * CHUNK + e
            right = turned[pl.ds(d, 48, stride=32), :].astype(BF16)
            rights.append(jnp.concatenate([right, right], axis=1))
            wh, wl = split(outer_ref[pl.ds(d, 32, stride=32), :])
            for k in range(2):
                at = (pl.ds(e * 64 + 32 * k, 32), pl.ds(k * LANES, LANES))
                spread_h[at] = wh
                spread_l[at] = wl
        product = dot(jnp.concatenate(rights, axis=0), left4)
        rows = []
        for g in range(6):
            halves = [[], []]
            for e in range(0, CHUNK, 2):
                lanes = slice(g * LANES, (g + 1) * LANES)
                first = product[e * 48 : (e + 1) * 48, lanes]
                second = product[(e + 1) * 48 : (e + 2) * 48, lanes]
                halves[0].append(jnp.where(low_lanes, first, pltpu.roll(second, 64, 1)))
                halves[1].append(jnp.where(low_lanes, pltpu.roll(first, 64, 1), second))
            rows += [jnp.concatenate(half, axis=1) for half in halves]
        ah, al = split(jnp.concatenate(rows, axis=0))
        bh, bl = spread_h[...], spread_l[...]
        step = dot(
            jnp.concatenate([ah, ah, al], axis=1), jnp.concatenate([bh, bl, bh], axis=0)
        )
        if t == 0:
            total[...] = step
        else:
            total[...] += step
    fetch.wait()
    for g in range(6):
        for k in range(4):
            start = (g * 2 + k // 2) * 48
            out_ref[g * 4 + k] = (
                state_ref[g * 4 + k]
                + total[start : start + 48, (k % 2) * LANES : (k % 2 + 1) * LANES]
                + bias_ref[...]
            )


def copies(value, axis):
    return jnp.broadcast_to(value[None], (lax.axis_size(axis), *value.shape))


def everyone(value, axis):
    return lax.all_to_all(copies(value, axis), axis, 0, 0, tiled=True)


def mirrored():
    sides = [((a, b), (b, a)) for a in range(4) for b in range(a + 1, 4)]
    sides += [((a, a), (a + 1, a + 1)) for a in (0, 2)]

    def index(y, zh, core, zl, x):
        return (((y * 4 + zh) * 2 + core) * 4 + zl) * 4 + x

    return [
        [index(y, zh, core, zl, x) for y, zl in pair for zh in range(4)]
        for core in range(2)
        for x in range(4)
        for pair in sides
    ]


VMEM = pl.BlockSpec(memory_space=pltpu.VMEM)
HBM = pl.BlockSpec(memory_space=pltpu.HBM)
PREPARE = pltpu.CompilerParams(vmem_limit_bytes=62 * 1024 * 1024)
PARAMS = pltpu.CompilerParams(vmem_limit_bytes=48 * 1024 * 1024)


def shape(*dims):
    return jax.ShapeDtypeStruct(dims, F32)


def first_exchange(alignment, pair_weights, align_gain):
    normed = pl.pallas_call(
        features_kernel, out_shape=shape(4, 48, 128), compiler_params=PREPARE
    )(alignment, align_gain)
    packed = pl.pallas_call(
        weights_kernel, out_shape=shape(16, 72, 128), compiler_params=PREPARE
    )(pair_weights)
    near = lax.all_to_all(normed, "zh", 0, 0, tiled=True).reshape(192, 128)
    near, packed = lax.optimization_barrier((near, packed))
    weights = lax.all_to_all(packed, COL, 0, 0, tiled=True)
    gathered = lax.all_gather(near, ("y", "core"), axis=0, tiled=True).reshape(32, 48, 128)
    return gathered, weights


def on_device(
    alignment,
    pair_state,
    pair_weights,
    align_gain,
    value_weight,
    gate_weight,
    output_weight,
    outer_gain,
    left_weight,
    right_weight,
    outer_weight,
    outer_bias,
):
    align_gain, outer_gain = align_gain[None], outer_gain[None]
    gathered, weights = first_exchange(alignment, pair_weights, align_gain)
    params = (
        alignment,
        value_weight,
        gate_weight,
        output_weight.T,
        left_weight.T,
        right_weight.T,
        align_gain,
        outer_gain,
    )
    alignment_out, left, right = pl.pallas_call(
        average_kernel,
        in_specs=[VMEM, VMEM] + [HBM] * len(params),
        out_specs=[VMEM] * 3,
        out_shape=(shape(24, 4, 64), shape(16, 24, 128), shape(8, 24, 128)),
        scratch_shapes=[pltpu.VMEM(p.shape, F32) for p in params]
        + [
            pltpu.VMEM((96, 128), F32),
            pltpu.VMEM((96, 128), F32),
            pltpu.SemaphoreType.DMA((len(params),)),
        ],
        compiler_params=PARAMS,
    )(weights, gathered, *params)
    right = lax.all_to_all(right, ALL, 0, 0, axis_index_groups=mirrored(), tiled=True)
    y, zl = lax.axis_index("y"), lax.axis_index("zl")
    side = jnp.where(y == zl, y % 2, jnp.where(y < zl, 1, 0))
    right = lax.dynamic_slice_in_dim(right, side * 4, 4, axis=0)
    right = jnp.broadcast_to(right[None], (4, *right.shape)).reshape(16, 24, 128)
    right = lax.all_to_all(right, ("y", "x"), 0, 0, tiled=True).reshape(384, 128)
    right, left = lax.optimization_barrier((right, left))
    left_all = lax.all_to_all(left, COL, 0, 0, tiled=True).reshape(384, 128)
    right_all = lax.all_gather(right, "core", axis=0, tiled=True)
    pair_out = pl.pallas_call(
        outer_kernel,
        in_specs=[VMEM] * 4 + [HBM],
        out_specs=VMEM,
        out_shape=shape(24, 48, 128),
        scratch_shapes=[
            pltpu.VMEM((1536, 128), F32),
            pltpu.VMEM((CHUNK * 64, 256), BF16),
            pltpu.VMEM((CHUNK * 64, 256), BF16),
            pltpu.VMEM((576, 256), F32),
            pltpu.VMEM((1, 128), F32),
            pltpu.SemaphoreType.DMA(()),
        ],
        compiler_params=PARAMS,
    )(left_all, right_all, pair_state, outer_weight, outer_bias[None])
    return alignment_out, pair_out


def solution(mesh):
    torus = Mesh(mesh.devices.reshape(4, 4, 2, 4, 4), ALL)
    return jax.shard_map(
        on_device,
        mesh=torus,
        in_specs=(P(ROW, COL, None), P(ROW, COL, None), P(None, ROW, COL)) + (P(),) * 9,
        out_specs=(P(ROW, COL, None), P(ROW, COL, None)),
        check_vma=False,
    )
```

```python
import functools

import jax
import jax.numpy as jnp
from jax import lax
from jax.experimental import pallas as pl
from jax.experimental.pallas import tpu as pltpu
from jax.sharding import Mesh, PartitionSpec as P

F32 = jnp.float32
BF16 = jnp.bfloat16
ROW = ("y", "zh", "core")
COL = ("zl", "x")
ALL = ROW + COL
LANES = 128
HALVES = (slice(0, 64), slice(64, 128))


def split(value):
    high = value.astype(BF16)
    low = (value - high.astype(F32)).astype(BF16)
    return high, low


def dot(a, b):
    return jnp.dot(a, b, preferred_element_type=F32)


def dot3(a, b):
    ah, al = split(a)
    bh, bl = split(b)
    return dot(ah, bh) + (dot(ah, bl) + dot(al, bh))


def normalize(features, gain):
    mean = jnp.mean(features, axis=-1, keepdims=True)
    centered = features - mean
    spread = jnp.mean(centered * centered, axis=-1, keepdims=True)
    return centered * lax.rsqrt(spread + 1e-05) * gain


def twice(weight):
    zeros = jnp.zeros_like(weight)
    return jnp.concatenate(
        [jnp.concatenate([weight, zeros], 1), jnp.concatenate([zeros, weight], 1)], 0
    )


def fill(ref, value):
    if len(ref.shape) == 2:
        ref[...] = value
    else:
        for k in range(ref.shape[0]):
            ref[k] = value


def features_kernel(align_ref, gain_ref, normed_ref):
    parts = [normalize(align_ref[:, s, :], gain_ref[...]) for s in range(4)]
    features = jnp.concatenate(
        [jnp.concatenate(parts[0:2], axis=1), jnp.concatenate(parts[2:4], axis=1)], axis=0
    )
    fill(normed_ref, features)


def weights_kernel(pair_w_ref, align_gain_ref, outer_gain_ref, bias_ref, weights_ref, small_ref):
    heads, rows, columns = pair_w_ref.shape
    turned = pair_w_ref[...].reshape(heads * rows, columns).T
    half = columns // 2
    tail = turned[:, LANES:]
    tail = jnp.concatenate([tail[:half], tail[half:]], axis=1)
    fill(weights_ref, jnp.concatenate([turned[:, :LANES], tail], axis=0))
    small_ref[0:1, 0:64] = align_gain_ref[...]
    small_ref[1:2, 0:64] = outer_gain_ref[...]
    small_ref[2:3, :] = bias_ref[...]


def dot3_turned(a, b):
    ah, al = split(a)
    bh, bl = split(b)

    def one(x, y):
        return lax.dot_general(x, y, (((1,), (1,)), ((), ())), preferred_element_type=F32)

    return one(ah, bh) + (one(ah, bl) + one(al, bh))


def landed(row):
    y, zh, core = row // 8, row // 2 % 4, row % 2
    return (y * 2 + core) * 4 + zh


def average_kernel(
    weights_ref,
    gathered_ref,
    small_ref,
    align_hbm,
    value_hbm,
    gate_hbm,
    output_hbm,
    left_hbm,
    right_hbm,
    out_ref,
    left_ref,
    right_ref,
    align_ref,
    value_ref,
    gate_ref,
    output_ref,
    left_w_ref,
    right_w_ref,
    left_tmp,
    right_tmp,
    arrived,
):
    fetches = [
        pltpu.make_async_copy(source, target, arrived.at[n])
        for n, (source, target) in enumerate(
            [
                (value_hbm, value_ref),
                (align_hbm, align_ref),
                (gate_hbm, gate_ref),
                (output_hbm, output_ref),
                (left_hbm, left_w_ref),
                (right_hbm, right_w_ref),
            ]
        )
    ]
    for fetch in fetches:
        fetch.start()
    rows = align_ref.shape[0]
    columns = 2 * rows
    heads = 8
    first = weights_ref[:, 0:columns, :].reshape(-1, LANES)
    tails = [weights_ref[k, columns:, :] for k in range(16)]
    second = jnp.concatenate([t[:, half] for t in tails for half in HALVES], axis=0)
    weights = jnp.concatenate([first.T, second.T], axis=0)
    wh, wl = split(weights)
    mixed = []
    for p in range(2):
        blocks = [
            gathered_ref[landed(r), p * rows : (p + 1) * rows, :] for r in range(32)
        ]
        fh, fl = split(jnp.concatenate(blocks, axis=0))
        mixed.append(dot(wh, fh) + (dot(wh, fl) + dot(wl, fh)))
    for fetch in fetches:
        fetch.wait()
    lane = lax.broadcasted_iota(jnp.int32, (rows, 512), 1)
    lane_head = lax.rem(lax.div(lane, 32), heads)
    vh, vl = split(twice(value_ref[...]))
    gate2 = twice(gate_ref[...])
    own = [normalize(align_ref[:, s, :], small_ref[0:1, 0:64]) for s in range(4)]
    gated = []
    for p in range(2):
        mh, ml = split(mixed[p])
        by_head = dot(mh, vh) + (dot(mh, vl) + dot(ml, vh))
        averaged = jnp.zeros((rows, 512), F32)
        for h in range(heads):
            averaged += jnp.where(lane_head == h, by_head[h * rows : (h + 1) * rows], 0.0)
        gate = jax.nn.sigmoid(dot3(jnp.concatenate(own[2 * p : 2 * p + 2], axis=1), gate2))
        product = gate * averaged
        gated += [product[:, :256], product[:, 256:]]
    update = dot3_turned(jnp.concatenate(gated, axis=0), output_ref[...])
    aligned = jnp.concatenate([align_ref[:, s, :] for s in range(4)], axis=0) + update
    for s in range(4):
        out_ref[:, s, :] = aligned[s * rows : (s + 1) * rows]
    normed = normalize(aligned, small_ref[1:2, 0:64])
    left_tmp[:, 0:32] = dot3_turned(normed, left_w_ref[...])
    right_tmp[:, 0:32] = dot3_turned(normed, right_w_ref[...])
    left = jnp.concatenate(
        [left_tmp[pl.ds(k, rows, stride=4), 0:32] for k in range(4)], axis=1
    )
    right = jnp.concatenate(
        [right_tmp[pl.ds(k, rows, stride=4), 0:32] for k in range(4)], axis=1
    )
    fill(left_ref, left)
    fill(right_ref, right)


CHUNK = 8


def outer_kernel(
    left_ref,
    right_ref,
    state_ref,
    outer_ref,
    small_ref,
    out_ref,
    turned,
    spread_h,
    spread_l,
    total,
):
    lefts = [left_ref[pl.ds(g, 64, stride=6), :] * (1.0 / 64.0) for g in range(6)]
    lh, ll = split(jnp.concatenate(lefts, axis=1))
    left4 = jnp.concatenate([lh, lh, ll, ll], axis=0)
    for core in range(2):
        for g in range(6):
            block = jnp.concatenate(
                [
                    right_ref[pl.ds((y * 2 + core) * 96 + g, 16, stride=6), :]
                    for y in range(4)
                ],
                axis=0,
            )
            high = block.astype(BF16).astype(F32)
            stacked = jnp.concatenate([high, block - high], axis=0)
            turned[(core * 6 + g) * LANES : (core * 6 + g + 1) * LANES, :] = stacked.T
    spread_h[...] = jnp.zeros_like(spread_h)
    spread_l[...] = jnp.zeros_like(spread_l)
    low_lanes = lax.broadcasted_iota(jnp.int32, (48, LANES), 1) < 64
    for t in range(32 // CHUNK):
        rights = []
        for e in range(CHUNK):
            d = t * CHUNK + e
            right = turned[pl.ds(d, 48, stride=32), :].astype(BF16)
            rights.append(jnp.concatenate([right, right], axis=1))
            wh, wl = split(outer_ref[pl.ds(d, 32, stride=32), :])
            for k in range(2):
                at = (pl.ds(e * 64 + 32 * k, 32), pl.ds(k * LANES, LANES))
                spread_h[at] = wh
                spread_l[at] = wl
        product = dot(jnp.concatenate(rights, axis=0), left4)
        rows = []
        for g in range(6):
            halves = [[], []]
            for e in range(0, CHUNK, 2):
                lanes = slice(g * LANES, (g + 1) * LANES)
                first = product[e * 48 : (e + 1) * 48, lanes]
                second = product[(e + 1) * 48 : (e + 2) * 48, lanes]
                halves[0].append(jnp.where(low_lanes, first, pltpu.roll(second, 64, 1)))
                halves[1].append(jnp.where(low_lanes, pltpu.roll(first, 64, 1), second))
            rows += [jnp.concatenate(half, axis=1) for half in halves]
        ah, al = split(jnp.concatenate(rows, axis=0))
        bh, bl = spread_h[...], spread_l[...]
        step = dot(
            jnp.concatenate([ah, ah, al], axis=1), jnp.concatenate([bh, bl, bh], axis=0)
        )
        if t == 0:
            total[...] = step
        else:
            total[...] += step
    for g in range(6):
        for k in range(4):
            start = (g * 2 + k // 2) * 48
            out_ref[g * 4 + k] = (
                state_ref[g * 4 + k]
                + total[start : start + 48, (k % 2) * LANES : (k % 2 + 1) * LANES]
                + small_ref[2:3, :]
            )


def copies(value, axis):
    return jnp.broadcast_to(value[None], (lax.axis_size(axis), *value.shape))


def everyone(value, axis):
    return lax.all_to_all(copies(value, axis), axis, 0, 0, tiled=True)


def mirrored():
    sides = [((a, b), (b, a)) for a in range(4) for b in range(a + 1, 4)]
    sides += [((a, a), (a + 1, a + 1)) for a in (0, 2)]

    def index(y, zh, core, zl, x):
        return (((y * 4 + zh) * 2 + core) * 4 + zl) * 4 + x

    return [
        [index(y, zh, core, zl, x) for y, zl in pair for zh in range(4)]
        for core in range(2)
        for x in range(4)
        for pair in sides
    ]


VMEM = pl.BlockSpec(memory_space=pltpu.VMEM)
HBM = pl.BlockSpec(memory_space=pltpu.HBM)
PREPARE = pltpu.CompilerParams(vmem_limit_bytes=62 * 1024 * 1024)
PARAMS = pltpu.CompilerParams(vmem_limit_bytes=48 * 1024 * 1024)


def shape(*dims):
    return jax.ShapeDtypeStruct(dims, F32)


def first_exchange(alignment, pair_weights, align_gain, outer_gain, outer_bias):
    normed = pl.pallas_call(
        features_kernel, out_shape=shape(4, 48, 128), compiler_params=PREPARE
    )(alignment, align_gain)
    packed, small = pl.pallas_call(
        weights_kernel, out_shape=(shape(16, 72, 128), shape(8, 128)), compiler_params=PARAMS
    )(pair_weights, align_gain, outer_gain, outer_bias)
    near = lax.all_to_all(normed, "zh", 0, 0, tiled=True).reshape(192, 128)
    near, packed = lax.optimization_barrier((near, packed))
    weights = lax.all_to_all(packed, COL, 0, 0, tiled=True)
    gathered = lax.all_gather(near, ("y", "core"), axis=0, tiled=True).reshape(32, 48, 128)
    return gathered, weights, small


def on_device(
    alignment,
    pair_state,
    pair_weights,
    align_gain,
    value_weight,
    gate_weight,
    output_weight,
    outer_gain,
    left_weight,
    right_weight,
    outer_weight,
    outer_bias,
):
    align_gain, outer_gain = align_gain[None], outer_gain[None]
    gathered, weights, small = first_exchange(
        alignment, pair_weights, align_gain, outer_gain, outer_bias[None]
    )
    params = (
        alignment,
        value_weight,
        gate_weight,
        output_weight.T,
        left_weight.T,
        right_weight.T,
    )
    alignment_out, left, right = pl.pallas_call(
        average_kernel,
        in_specs=[VMEM] * 3 + [HBM] * len(params),
        out_specs=[VMEM] * 3,
        out_shape=(shape(24, 4, 64), shape(24, 128), shape(8, 24, 128)),
        scratch_shapes=[pltpu.VMEM(p.shape, F32) for p in params]
        + [
            pltpu.VMEM((96, 128), F32),
            pltpu.VMEM((96, 128), F32),
            pltpu.SemaphoreType.DMA((len(params),)),
        ],
        compiler_params=PARAMS,
    )(weights, gathered, small, *params)
    right = lax.all_to_all(right, ALL, 0, 0, axis_index_groups=mirrored(), tiled=True)
    left = lax.all_gather(left, "x", axis=0, tiled=True)
    right, left = lax.optimization_barrier((right, left))
    y, zl = lax.axis_index("y"), lax.axis_index("zl")
    side = jnp.where(y == zl, y % 2, jnp.where(y < zl, 1, 0))
    right = lax.dynamic_slice_in_dim(right, side * 4, 4, axis=0)
    right = jnp.broadcast_to(right[None], (8, *right.shape)).reshape(32, 24, 128)
    right_all = lax.all_to_all(right, ("y", "core", "x"), 0, 0, tiled=True)
    right_all = right_all.reshape(768, 128)
    left_all = lax.all_gather(left, "zl", axis=0, tiled=True)
    pair_out = pl.pallas_call(
        outer_kernel,
        out_shape=shape(24, 48, 128),
        scratch_shapes=[
            pltpu.VMEM((1536, 128), F32),
            pltpu.VMEM((CHUNK * 64, 256), BF16),
            pltpu.VMEM((CHUNK * 64, 256), BF16),
            pltpu.VMEM((576, 256), F32),
        ],
        compiler_params=PARAMS,
    )(left_all, right_all, pair_state, outer_weight, small)
    return alignment_out, pair_out


def solution(mesh):
    torus = Mesh(mesh.devices.reshape(4, 4, 2, 4, 4), ALL)
    return jax.shard_map(
        on_device,
        mesh=torus,
        in_specs=(P(ROW, COL, None), P(ROW, COL, None), P(None, ROW, COL)) + (P(),) * 9,
        out_specs=(P(ROW, COL, None), P(ROW, COL, None)),
        check_vma=False,
    )
```

```python
import functools

import jax
import jax.numpy as jnp
from jax import lax
from jax.experimental import pallas as pl
from jax.experimental.pallas import tpu as pltpu
from jax.sharding import Mesh, PartitionSpec as P

F32 = jnp.float32
BF16 = jnp.bfloat16
ROW = ("y", "zh", "core")
COL = ("zl", "x")
ALL = ROW + COL
LANES = 128
HALVES = (slice(0, 64), slice(64, 128))


def split(value):
    high = value.astype(BF16)
    low = (value - high.astype(F32)).astype(BF16)
    return high, low


def dot(a, b):
    return jnp.dot(a, b, preferred_element_type=F32)


def dot3(a, b):
    ah, al = split(a)
    bh, bl = split(b)
    return dot(ah, bh) + (dot(ah, bl) + dot(al, bh))


def normalize(features, gain):
    mean = jnp.mean(features, axis=-1, keepdims=True)
    centered = features - mean
    spread = jnp.mean(centered * centered, axis=-1, keepdims=True)
    return centered * lax.rsqrt(spread + 1e-05) * gain


def twice(weight):
    zeros = jnp.zeros_like(weight)
    return jnp.concatenate(
        [jnp.concatenate([weight, zeros], 1), jnp.concatenate([zeros, weight], 1)], 0
    )


def fill(ref, value):
    if len(ref.shape) == 2:
        ref[...] = value
    else:
        for k in range(ref.shape[0]):
            ref[k] = value


def features_kernel(align_ref, gain_ref, normed_ref):
    parts = [normalize(align_ref[:, s, :], gain_ref[...]) for s in range(4)]
    features = jnp.concatenate(
        [jnp.concatenate(parts[0:2], axis=1), jnp.concatenate(parts[2:4], axis=1)], axis=0
    )
    fill(normed_ref, features)


def early_kernel(
    pair_w_ref,
    align_ref,
    gate_w_ref,
    outer_ref,
    align_gain_ref,
    outer_gain_ref,
    bias_ref,
    weights_ref,
    gate_ref,
    spread_ref,
    small_ref,
):
    heads, rows, columns = pair_w_ref.shape
    turned = pair_w_ref[...].reshape(heads * rows, columns).T
    half = columns // 2
    tail = turned[:, LANES:]
    tail = jnp.concatenate([tail[:half], tail[half:]], axis=1)
    fill(weights_ref, jnp.concatenate([turned[:, :LANES], tail], axis=0))
    small_ref[0:1, 0:64] = outer_gain_ref[...]
    small_ref[1:2, :] = bias_ref[...]
    own = [normalize(align_ref[:, s, :], align_gain_ref[...]) for s in range(4)]
    logits = dot3(jnp.concatenate(own, axis=0), gate_w_ref[...])
    for s in range(4):
        gate_ref[:, s * 256 : (s + 1) * 256] = jax.nn.sigmoid(logits[s * rows : (s + 1) * rows])
    for d in range(32):
        wh, wl = split(outer_ref[pl.ds(d, 32, stride=32), :])
        both = jnp.concatenate([wh, wl], axis=1)
        spread_ref[pl.ds(d * 32, 32), :] = both
        spread_ref[pl.ds(1024 + d * 32, 32), :] = both


def copies_kernel(blocks_ref, out_ref):
    block = blocks_ref[0:4] + blocks_ref[4:8]
    for k in range(8):
        out_ref[4 * k : 4 * k + 4] = block


def dot3_turned(a, b):
    ah, al = split(a)
    bh, bl = split(b)

    def one(x, y):
        return lax.dot_general(x, y, (((1,), (1,)), ((), ())), preferred_element_type=F32)

    return one(ah, bh) + (one(ah, bl) + one(al, bh))


def landed(row):
    y, zh, core = row // 8, row // 2 % 4, row % 2
    return (y * 2 + core) * 4 + zh


def average_kernel(
    weights_ref,
    gathered_ref,
    gate_ref,
    small_ref,
    align_ref,
    value_ref,
    output_ref,
    left_w_ref,
    right_w_ref,
    out_ref,
    left_ref,
    right_ref,
    left_tmp,
    right_tmp,
):
    rows = align_ref.shape[0]
    columns = 2 * rows
    heads = 8
    first = weights_ref[:, 0:columns, :].reshape(-1, LANES)
    tails = [weights_ref[k, columns:, :] for k in range(16)]
    second = jnp.concatenate([t[:, half] for t in tails for half in HALVES], axis=0)
    weights = jnp.concatenate([first.T, second.T], axis=0)
    wh, wl = split(weights)
    mixed = []
    for p in range(2):
        blocks = [
            gathered_ref[landed(r), p * rows : (p + 1) * rows, :] for r in range(32)
        ]
        fh, fl = split(jnp.concatenate(blocks, axis=0))
        mixed.append(dot(wh, fh) + (dot(wh, fl) + dot(wl, fh)))
    lane = lax.broadcasted_iota(jnp.int32, (rows, 512), 1)
    lane_head = lax.rem(lax.div(lane, 32), heads)
    vh, vl = split(twice(value_ref[...]))
    gated = []
    for p in range(2):
        mh, ml = split(mixed[p])
        by_head = dot(mh, vh) + (dot(mh, vl) + dot(ml, vh))
        averaged = jnp.zeros((rows, 512), F32)
        for h in range(heads):
            averaged += jnp.where(lane_head == h, by_head[h * rows : (h + 1) * rows], 0.0)
        product = gate_ref[:, p * 512 : (p + 1) * 512] * averaged
        gated += [product[:, :256], product[:, 256:]]
    update = dot3_turned(jnp.concatenate(gated, axis=0), output_ref[...])
    aligned = jnp.concatenate([align_ref[:, s, :] for s in range(4)], axis=0) + update
    for s in range(4):
        out_ref[:, s, :] = aligned[s * rows : (s + 1) * rows]
    normed = normalize(aligned, small_ref[0:1, 0:64])
    left_tmp[:, 0:32] = dot3_turned(normed, left_w_ref[...])
    right_tmp[:, 0:32] = dot3_turned(normed, right_w_ref[...])
    left = jnp.concatenate(
        [left_tmp[pl.ds(k, rows, stride=4), 0:32] for k in range(4)], axis=1
    )
    right = jnp.concatenate(
        [right_tmp[pl.ds(k, rows, stride=4), 0:32] for k in range(4)], axis=1
    )
    fill(left_ref, left)
    y, zl = lax.axis_index("y"), lax.axis_index("zl")
    side = jnp.where(y == zl, lax.rem(y, 2), jnp.where(y < zl, 1, 0))
    for k in range(8):
        right_ref[k] = jnp.where(side == k // 4, right, 0.0)


CHUNK = 8


def outer_kernel(
    left_ref, right_ref, state_ref, spread_ref, small_ref, out_ref, turned
):
    lefts = [left_ref[pl.ds(g, 64, stride=6), :] * (1.0 / 64.0) for g in range(6)]
    lh, ll = split(jnp.concatenate(lefts, axis=1))
    left4 = jnp.concatenate([lh, lh, ll, ll], axis=0)
    for core in range(2):
        for g in range(6):
            block = jnp.concatenate(
                [
                    right_ref[pl.ds((y * 2 + core) * 96 + g, 16, stride=6), :]
                    for y in range(4)
                ],
                axis=0,
            )
            high = block.astype(BF16).astype(F32)
            stacked = jnp.concatenate([high, block - high], axis=0)
            turned[(core * 6 + g) * LANES : (core * 6 + g + 1) * LANES, :] = stacked.T
    rights = []
    for d in range(32):
        right = turned[pl.ds(d, 48, stride=32), :].astype(BF16)
        rights.append(jnp.concatenate([right, right], axis=1))
    right4 = jnp.concatenate(rights, axis=0)
    lane = lax.broadcasted_iota(jnp.int32, (48, LANES), 1)
    low_half = lane < 64
    even = lax.rem(lax.div(lane, 32), 2) == 0

    def exchange(a, b, shift, keep):
        return (
            jnp.where(keep, a, pltpu.roll(b, shift, 1)),
            jnp.where(keep, pltpu.roll(a, LANES - shift, 1), b),
        )

    for pair in range(6 // 6):
        product = dot(right4, left4[:, pair * 6 * LANES : (pair + 1) * 6 * LANES])
        rows = []
        for g in range(6):
            lanes = slice(g * LANES, (g + 1) * LANES)
            pieces = [[], [], [], []]
            for t in range(0, 32, 4):
                p0, p1, p2, p3 = (
                    product[(t + e) * 48 : (t + e + 1) * 48, lanes] for e in range(4)
                )
                a0, a2 = exchange(p0, p2, 64, low_half)
                a1, a3 = exchange(p1, p3, 64, low_half)
                k0, k1 = exchange(a0, a1, 32, even)
                k2, k3 = exchange(a2, a3, 32, even)
                for k, piece in enumerate((k0, k1, k2, k3)):
                    pieces[k].append(piece)
            rows += [jnp.concatenate(piece, axis=1) for piece in pieces]
        ah, al = split(jnp.concatenate(rows, axis=0))
        update = dot(jnp.concatenate([ah, al], axis=1), spread_ref[...])
        for n in range(4 * 6):
            i = pair * 4 * 6 + n
            part = update[n * 48 : (n + 1) * 48]
            out_ref[i] = (
                state_ref[i] + (part[:, :LANES] + part[:, LANES:]) + small_ref[1:2, :]
            )


def mirrored():
    sides = [((a, b), (b, a)) for a in range(4) for b in range(a + 1, 4)]
    sides += [((a, a), (a + 1, a + 1)) for a in (0, 2)]

    def index(y, zh, core, zl, x):
        return (((y * 4 + zh) * 2 + core) * 4 + zl) * 4 + x

    return [
        [index(y, zh, core, zl, x) for y, zl in pair for zh in range(4)]
        for core in range(2)
        for x in range(4)
        for pair in sides
    ]


PREPARE = pltpu.CompilerParams(vmem_limit_bytes=62 * 1024 * 1024)
PARAMS = pltpu.CompilerParams(vmem_limit_bytes=48 * 1024 * 1024)


OUTER_SCRATCH = [pltpu.VMEM((1536, 128), F32)]


def shape(*dims):
    return jax.ShapeDtypeStruct(dims, F32)


def on_device(
    alignment,
    pair_state,
    pair_weights,
    align_gain,
    value_weight,
    gate_weight,
    output_weight,
    outer_gain,
    left_weight,
    right_weight,
    outer_weight,
    outer_bias,
):
    align_gain, outer_gain = align_gain[None], outer_gain[None]
    normed = pl.pallas_call(
        features_kernel, out_shape=shape(4, 48, 128), compiler_params=PREPARE
    )(alignment, align_gain)
    packed, gate, spread, small = pl.pallas_call(
        early_kernel,
        out_shape=(
            shape(16, 72, 128),
            shape(24, 1024),
            jax.ShapeDtypeStruct((2048, 256), BF16),
            shape(8, 128),
        ),
        compiler_params=PARAMS,
    )(
        pair_weights,
        alignment,
        gate_weight,
        outer_weight,
        align_gain,
        outer_gain,
        outer_bias[None],
    )
    near = lax.all_to_all(normed, "zh", 0, 0, tiled=True).reshape(192, 128)
    near, packed = lax.optimization_barrier((near, packed))
    weights = lax.all_to_all(packed, COL, 0, 0, tiled=True)
    gathered = lax.all_gather(near, ("y", "core"), axis=0, tiled=True).reshape(32, 48, 128)
    alignment_out, left, right = pl.pallas_call(
        average_kernel,
        out_shape=(shape(24, 4, 64), shape(24, 128), shape(8, 24, 128)),
        scratch_shapes=[pltpu.VMEM((96, 128), F32), pltpu.VMEM((96, 128), F32)],
        compiler_params=PARAMS,
    )(
        weights,
        gathered,
        gate,
        small,
        alignment,
        value_weight,
        output_weight.T,
        left_weight.T,
        right_weight.T,
    )
    right = lax.all_to_all(right, ALL, 0, 0, axis_index_groups=mirrored(), tiled=True)
    left = lax.all_gather(left, "x", axis=0, tiled=True)
    right, left = lax.optimization_barrier((right, left))
    right = pl.pallas_call(
        copies_kernel, out_shape=shape(32, 24, 128), compiler_params=PARAMS
    )(right)
    right_all = lax.all_to_all(right, ("y", "core", "x"), 0, 0, tiled=True)
    right_all = right_all.reshape(768, 128)
    left_all = lax.all_gather(left, "zl", axis=0, tiled=True)
    pair_out = pl.pallas_call(
        outer_kernel,
        out_shape=shape(24, 48, 128),
        scratch_shapes=OUTER_SCRATCH,
        compiler_params=PARAMS,
    )(left_all, right_all, pair_state, spread, small)
    return alignment_out, pair_out


def solution(mesh):
    torus = Mesh(mesh.devices.reshape(4, 4, 2, 4, 4), ALL)
    return jax.shard_map(
        on_device,
        mesh=torus,
        in_specs=(P(ROW, COL, None), P(ROW, COL, None), P(None, ROW, COL)) + (P(),) * 9,
        out_specs=(P(ROW, COL, None), P(ROW, COL, None)),
        check_vma=False,
    )
```

```python
import functools

import jax
import jax.numpy as jnp
from jax import lax
from jax.experimental import pallas as pl
from jax.experimental.pallas import tpu as pltpu
from jax.sharding import Mesh, PartitionSpec as P

F32 = jnp.float32
BF16 = jnp.bfloat16
ROW = ("y", "zh", "core")
COL = ("zl", "x")
ALL = ROW + COL
FAR = (2, 3, 0, 1)
RING = (0, 2, 3, 1)
MIDDLE = (5, *range(5), *range(6, 16))
LANES = 128
HALVES = (slice(0, 64), slice(64, 128))


def split(value):
    high = value.astype(BF16)
    low = (value - high.astype(F32)).astype(BF16)
    return high, low


def dot(a, b):
    return jnp.dot(a, b, preferred_element_type=F32)


def dot3(a, b):
    ah, al = split(a)
    bh, bl = split(b)
    return dot(ah, bh) + (dot(ah, bl) + dot(al, bh))


def normalize(features, gain):
    mean = jnp.mean(features, axis=-1, keepdims=True)
    centered = features - mean
    spread = jnp.mean(centered * centered, axis=-1, keepdims=True)
    return centered * lax.rsqrt(spread + 1e-05) * gain


def twice(weight):
    zeros = jnp.zeros_like(weight)
    return jnp.concatenate(
        [jnp.concatenate([weight, zeros], 1), jnp.concatenate([zeros, weight], 1)], 0
    )


def fill(ref, value):
    if len(ref.shape) == 2:
        ref[...] = value
    else:
        for k in range(ref.shape[0]):
            ref[k] = value


def features_kernel(align_ref, gain_ref, normed_ref):
    parts = [normalize(align_ref[:, s, :], gain_ref[...]) for s in range(4)]
    features = jnp.concatenate(
        [jnp.concatenate(parts[0:2], axis=1), jnp.concatenate(parts[2:4], axis=1)], axis=0
    )
    fill(normed_ref, features)


def early_kernel(
    pair_w_ref,
    align_ref,
    gate_w_ref,
    outer_ref,
    align_gain_ref,
    outer_gain_ref,
    bias_ref,
    weights_ref,
    gate_ref,
    spread_ref,
    small_ref,
):
    heads, rows, columns = pair_w_ref.shape
    turned = pair_w_ref[...].reshape(heads * rows, columns).T
    half = columns // 2
    tail = turned[:, LANES:]
    tail = jnp.concatenate([tail[:half], tail[half:]], axis=1)
    fill(weights_ref, jnp.concatenate([turned[:, :LANES], tail], axis=0))
    small_ref[0:1, 0:64] = outer_gain_ref[...]
    small_ref[1:2, :] = bias_ref[...]
    own = [normalize(align_ref[:, s, :], align_gain_ref[...]) for s in range(4)]
    logits = dot3(jnp.concatenate(own, axis=0), gate_w_ref[...])
    for s in range(4):
        gate_ref[:, s * 256 : (s + 1) * 256] = jax.nn.sigmoid(logits[s * rows : (s + 1) * rows])
    for d in range(32):
        wh, wl = split(outer_ref[pl.ds(d, 32, stride=32), :])
        both = jnp.concatenate([wh, wl], axis=1)
        spread_ref[pl.ds(d * 32, 32), :] = both
        spread_ref[pl.ds(1024 + d * 32, 32), :] = both


def copies_kernel(blocks_ref, out_ref):
    for x in range(4):
        at = FAR.index(x)
        block = blocks_ref[at] + blocks_ref[at + 4]
        for k in range(8):
            out_ref[4 * k + x] = block


def dot3_turned(a, b):
    ah, al = split(a)
    bh, bl = split(b)

    def one(x, y):
        return lax.dot_general(x, y, (((1,), (1,)), ((), ())), preferred_element_type=F32)

    return one(ah, bh) + (one(ah, bl) + one(al, bh))


def landed(row):
    y, zh, core = row // 8, row // 2 % 4, row % 2
    return (y * 2 + core) * 4 + FAR.index(zh)


def average_kernel(
    weights_ref,
    gathered_ref,
    gate_ref,
    small_ref,
    align_ref,
    value_ref,
    output_ref,
    left_w_ref,
    right_w_ref,
    out_ref,
    left_ref,
    right_ref,
    left_tmp,
    right_tmp,
):
    rows = align_ref.shape[0]
    columns = 2 * rows
    heads = 8
    order = [MIDDLE.index(c) for c in range(16)]
    first = jnp.concatenate([weights_ref[k, 0:columns, :] for k in order], axis=0)
    tails = [weights_ref[k, columns:, :] for k in order]
    second = jnp.concatenate([t[:, half] for t in tails for half in HALVES], axis=0)
    weights = jnp.concatenate([first.T, second.T], axis=0)
    wh, wl = split(weights)
    mixed = []
    for p in range(2):
        blocks = [
            gathered_ref[landed(r), p * rows : (p + 1) * rows, :] for r in range(32)
        ]
        fh, fl = split(jnp.concatenate(blocks, axis=0))
        mixed.append(dot(wh, fh) + (dot(wh, fl) + dot(wl, fh)))
    lane = lax.broadcasted_iota(jnp.int32, (rows, 512), 1)
    lane_head = lax.rem(lax.div(lane, 32), heads)
    vh, vl = split(twice(value_ref[...]))
    gated = []
    for p in range(2):
        mh, ml = split(mixed[p])
        by_head = dot(mh, vh) + (dot(mh, vl) + dot(ml, vh))
        averaged = jnp.zeros((rows, 512), F32)
        for h in range(heads):
            averaged += jnp.where(lane_head == h, by_head[h * rows : (h + 1) * rows], 0.0)
        product = gate_ref[:, p * 512 : (p + 1) * 512] * averaged
        gated += [product[:, :256], product[:, 256:]]
    update = dot3_turned(jnp.concatenate(gated, axis=0), output_ref[...])
    aligned = jnp.concatenate([align_ref[:, s, :] for s in range(4)], axis=0) + update
    for s in range(4):
        out_ref[:, s, :] = aligned[s * rows : (s + 1) * rows]
    normed = normalize(aligned, small_ref[0:1, 0:64])
    left_tmp[:, 0:32] = dot3_turned(normed, left_w_ref[...])
    right_tmp[:, 0:32] = dot3_turned(normed, right_w_ref[...])
    left = jnp.concatenate(
        [left_tmp[pl.ds(k, rows, stride=4), 0:32] for k in range(4)], axis=1
    )
    right = jnp.concatenate(
        [right_tmp[pl.ds(k, rows, stride=4), 0:32] for k in range(4)], axis=1
    )
    fill(left_ref, left)
    y, zl = lax.axis_index("y"), lax.axis_index("zl")
    side = jnp.where(y == zl, lax.rem(y, 2), jnp.where(y < zl, 1, 0))
    for k in range(8):
        right_ref[k] = jnp.where(side == k // 4, right, 0.0)


CHUNK = 8


def outer_kernel(
    left_ref, right_ref, state_ref, spread_ref, small_ref, out_ref, turned
):
    lefts = [left_ref[pl.ds(g, 64, stride=6), :] * (1.0 / 64.0) for g in range(6)]
    lh, ll = split(jnp.concatenate(lefts, axis=1))
    left4 = jnp.concatenate([lh, lh, ll, ll], axis=0)
    for core in range(2):
        for g in range(6):
            block = jnp.concatenate(
                [
                    right_ref[pl.ds((y * 2 + core) * 96 + g, 16, stride=6), :]
                    for y in RING
                ],
                axis=0,
            )
            high = block.astype(BF16).astype(F32)
            stacked = jnp.concatenate([high, block - high], axis=0)
            turned[(core * 6 + g) * LANES : (core * 6 + g + 1) * LANES, :] = stacked.T
    rights = []
    for d in range(32):
        right = turned[pl.ds(d, 48, stride=32), :].astype(BF16)
        rights.append(jnp.concatenate([right, right], axis=1))
    right4 = jnp.concatenate(rights, axis=0)
    lane = lax.broadcasted_iota(jnp.int32, (48, LANES), 1)
    low_half = lane < 64
    even = lax.rem(lax.div(lane, 32), 2) == 0

    def exchange(a, b, shift, keep):
        return (
            jnp.where(keep, a, pltpu.roll(b, shift, 1)),
            jnp.where(keep, pltpu.roll(a, LANES - shift, 1), b),
        )

    for pair in range(6 // 6):
        product = dot(right4, left4[:, pair * 6 * LANES : (pair + 1) * 6 * LANES])
        rows = []
        for g in range(6):
            lanes = slice(g * LANES, (g + 1) * LANES)
            pieces = [[], [], [], []]
            for t in range(0, 32, 4):
                p0, p1, p2, p3 = (
                    product[(t + e) * 48 : (t + e + 1) * 48, lanes] for e in range(4)
                )
                a0, a2 = exchange(p0, p2, 64, low_half)
                a1, a3 = exchange(p1, p3, 64, low_half)
                k0, k1 = exchange(a0, a1, 32, even)
                k2, k3 = exchange(a2, a3, 32, even)
                for k, piece in enumerate((k0, k1, k2, k3)):
                    pieces[k].append(piece)
            rows += [jnp.concatenate(piece, axis=1) for piece in pieces]
        ah, al = split(jnp.concatenate(rows, axis=0))
        update = dot(jnp.concatenate([ah, al], axis=1), spread_ref[...])
        for n in range(4 * 6):
            i = pair * 4 * 6 + n
            part = update[n * 48 : (n + 1) * 48]
            out_ref[i] = (
                state_ref[i] + (part[:, :LANES] + part[:, LANES:]) + small_ref[1:2, :]
            )


def mirrored():
    sides = [((a, b), (b, a)) for a in range(4) for b in range(a + 1, 4)]
    sides += [((a, a), (a + 1, a + 1)) for a in (0, 2)]

    def index(y, zh, core, zl, x):
        return (((y * 4 + zh) * 2 + core) * 4 + zl) * 4 + x

    return [
        [index(y, zh, core, zl, x) for y, zl in pair for zh in FAR]
        for core in range(2)
        for x in range(4)
        for pair in sides
    ]


PREPARE = pltpu.CompilerParams(vmem_limit_bytes=62 * 1024 * 1024)
PARAMS = pltpu.CompilerParams(vmem_limit_bytes=48 * 1024 * 1024)


OUTER_SCRATCH = [pltpu.VMEM((1536, 128), F32)]


def shape(*dims):
    return jax.ShapeDtypeStruct(dims, F32)


def on_device(
    alignment,
    pair_state,
    pair_weights,
    align_gain,
    value_weight,
    gate_weight,
    output_weight,
    outer_gain,
    left_weight,
    right_weight,
    outer_weight,
    outer_bias,
):
    align_gain, outer_gain = align_gain[None], outer_gain[None]
    normed = pl.pallas_call(
        features_kernel, out_shape=shape(4, 48, 128), compiler_params=PREPARE
    )(alignment, align_gain)
    packed, gate, spread, small = pl.pallas_call(
        early_kernel,
        out_shape=(
            shape(16, 72, 128),
            shape(24, 1024),
            jax.ShapeDtypeStruct((2048, 256), BF16),
            shape(8, 128),
        ),
        compiler_params=PARAMS,
    )(
        pair_weights,
        alignment,
        gate_weight,
        outer_weight,
        align_gain,
        outer_gain,
        outer_bias[None],
    )
    near = lax.all_to_all(
        normed, "zh", 0, 0, axis_index_groups=[list(FAR)], tiled=True
    ).reshape(192, 128)
    near, packed = lax.optimization_barrier((near, packed))
    weights = lax.all_to_all(packed, COL, 0, 0, axis_index_groups=[list(MIDDLE)], tiled=True)
    gathered = lax.all_gather(near, ("y", "core"), axis=0, tiled=True).reshape(32, 48, 128)
    alignment_out, left, right = pl.pallas_call(
        average_kernel,
        out_shape=(shape(24, 4, 64), shape(24, 128), shape(8, 24, 128)),
        scratch_shapes=[pltpu.VMEM((96, 128), F32), pltpu.VMEM((96, 128), F32)],
        compiler_params=PARAMS,
    )(
        weights,
        gathered,
        gate,
        small,
        alignment,
        value_weight,
        output_weight.T,
        left_weight.T,
        right_weight.T,
    )
    right = lax.all_to_all(right, ALL, 0, 0, axis_index_groups=mirrored(), tiled=True)
    left = lax.all_gather(left, "x", axis=0, tiled=True)
    right, left = lax.optimization_barrier((right, left))
    right = pl.pallas_call(
        copies_kernel, out_shape=shape(32, 24, 128), compiler_params=PARAMS
    )(right)
    right_all = lax.all_to_all(right, ("y", "core", "x"), 0, 0, tiled=True)
    right_all = right_all.reshape(768, 128)
    left_all = lax.all_gather(left, "zl", axis=0, axis_index_groups=[list(RING)], tiled=True)
    pair_out = pl.pallas_call(
        outer_kernel,
        out_shape=shape(24, 48, 128),
        scratch_shapes=OUTER_SCRATCH,
        compiler_params=PARAMS,
    )(left_all, right_all, pair_state, spread, small)
    return alignment_out, pair_out


def solution(mesh):
    torus = Mesh(mesh.devices.reshape(4, 4, 2, 4, 4), ALL)
    return jax.shard_map(
        on_device,
        mesh=torus,
        in_specs=(P(ROW, COL, None), P(ROW, COL, None), P(None, ROW, COL)) + (P(),) * 9,
        out_specs=(P(ROW, COL, None), P(ROW, COL, None)),
        check_vma=False,
    )
```

```python
import functools

import jax
import jax.numpy as jnp
from jax import lax
from jax.experimental import pallas as pl
from jax.experimental.pallas import tpu as pltpu
from jax.sharding import Mesh, PartitionSpec as P

F32 = jnp.float32
BF16 = jnp.bfloat16
ROW = ("y", "zh", "core")
COL = ("zl", "x")
ALL = ROW + COL
FAR = (2, 0, 3, 1)
RING = (0, 2, 3, 1)
MIDDLE = (6, *range(6), *range(7, 16))
LANES = 128
HALVES = (slice(0, 64), slice(64, 128))


def split(value):
    high = value.astype(BF16)
    low = (value - high.astype(F32)).astype(BF16)
    return high, low


def dot(a, b):
    return jnp.dot(a, b, preferred_element_type=F32)


def dot3(a, b):
    ah, al = split(a)
    bh, bl = split(b)
    return dot(ah, bh) + (dot(ah, bl) + dot(al, bh))


def normalize(features, gain):
    mean = jnp.mean(features, axis=-1, keepdims=True)
    centered = features - mean
    spread = jnp.mean(centered * centered, axis=-1, keepdims=True)
    return centered * lax.rsqrt(spread + 1e-05) * gain


def twice(weight):
    zeros = jnp.zeros_like(weight)
    return jnp.concatenate(
        [jnp.concatenate([weight, zeros], 1), jnp.concatenate([zeros, weight], 1)], 0
    )


def fill(ref, value):
    if len(ref.shape) == 2:
        ref[...] = value
    else:
        for k in range(ref.shape[0]):
            ref[k] = value


def features_kernel(align_ref, gain_ref, normed_ref):
    parts = [normalize(align_ref[:, s, :], gain_ref[...]) for s in range(4)]
    features = jnp.concatenate(
        [jnp.concatenate(parts[0:2], axis=1), jnp.concatenate(parts[2:4], axis=1)], axis=0
    )
    fill(normed_ref, features)


def early_kernel(
    pair_w_ref,
    align_ref,
    gate_w_ref,
    outer_ref,
    align_gain_ref,
    outer_gain_ref,
    bias_ref,
    weights_ref,
    gate_ref,
    spread_ref,
    small_ref,
):
    heads, rows, columns = pair_w_ref.shape
    turned = pair_w_ref[...].reshape(heads * rows, columns).T
    half = columns // 2
    tail = turned[:, LANES:]
    tail = jnp.concatenate([tail[:half], tail[half:]], axis=1)
    fill(weights_ref, jnp.concatenate([turned[:, :LANES], tail], axis=0))
    small_ref[0:1, 0:64] = outer_gain_ref[...]
    small_ref[1:2, :] = bias_ref[...]
    own = [normalize(align_ref[:, s, :], align_gain_ref[...]) for s in range(4)]
    logits = dot3(jnp.concatenate(own, axis=0), gate_w_ref[...])
    for s in range(4):
        gate_ref[:, s * 256 : (s + 1) * 256] = jax.nn.sigmoid(logits[s * rows : (s + 1) * rows])
    for d in range(32):
        wh, wl = split(outer_ref[pl.ds(d, 32, stride=32), :])
        both = jnp.concatenate([wh, wl], axis=1)
        spread_ref[pl.ds(d * 32, 32), :] = both
        spread_ref[pl.ds(1024 + d * 32, 32), :] = both


def copies_kernel(blocks_ref, out_ref):
    for x in range(4):
        at = FAR.index(x)
        block = blocks_ref[at] + blocks_ref[at + 4]
        for k in range(8):
            out_ref[4 * k + x] = block


def dot3_turned(a, b):
    ah, al = split(a)
    bh, bl = split(b)

    def one(x, y):
        return lax.dot_general(x, y, (((1,), (1,)), ((), ())), preferred_element_type=F32)

    return one(ah, bh) + (one(ah, bl) + one(al, bh))


def landed(row):
    y, zh, core = row // 8, row // 2 % 4, row % 2
    return (y * 2 + core) * 4 + FAR.index(zh)


def average_kernel(
    weights_ref,
    gathered_ref,
    gate_ref,
    small_ref,
    align_ref,
    value_ref,
    output_ref,
    left_w_ref,
    right_w_ref,
    out_ref,
    left_ref,
    right_ref,
    left_tmp,
    right_tmp,
):
    rows = align_ref.shape[0]
    columns = 2 * rows
    heads = 8
    order = [MIDDLE.index(c) for c in range(16)]
    first = jnp.concatenate([weights_ref[k, 0:columns, :] for k in order], axis=0)
    tails = [weights_ref[k, columns:, :] for k in order]
    second = jnp.concatenate([t[:, half] for t in tails for half in HALVES], axis=0)
    weights = jnp.concatenate([first.T, second.T], axis=0)
    wh, wl = split(weights)
    mixed = []
    for p in range(2):
        blocks = [
            gathered_ref[landed(r), p * rows : (p + 1) * rows, :] for r in range(32)
        ]
        fh, fl = split(jnp.concatenate(blocks, axis=0))
        mixed.append(dot(wh, fh) + (dot(wh, fl) + dot(wl, fh)))
    lane = lax.broadcasted_iota(jnp.int32, (rows, 512), 1)
    lane_head = lax.rem(lax.div(lane, 32), heads)
    vh, vl = split(twice(value_ref[...]))
    gated = []
    for p in range(2):
        mh, ml = split(mixed[p])
        by_head = dot(mh, vh) + (dot(mh, vl) + dot(ml, vh))
        averaged = jnp.zeros((rows, 512), F32)
        for h in range(heads):
            averaged += jnp.where(lane_head == h, by_head[h * rows : (h + 1) * rows], 0.0)
        product = gate_ref[:, p * 512 : (p + 1) * 512] * averaged
        gated += [product[:, :256], product[:, 256:]]
    update = dot3_turned(jnp.concatenate(gated, axis=0), output_ref[...])
    aligned = jnp.concatenate([align_ref[:, s, :] for s in range(4)], axis=0) + update
    for s in range(4):
        out_ref[:, s, :] = aligned[s * rows : (s + 1) * rows]
    normed = normalize(aligned, small_ref[0:1, 0:64])
    left_tmp[:, 0:32] = dot3_turned(normed, left_w_ref[...])
    right_tmp[:, 0:32] = dot3_turned(normed, right_w_ref[...])
    left = jnp.concatenate(
        [left_tmp[pl.ds(k, rows, stride=4), 0:32] for k in range(4)], axis=1
    )
    right = jnp.concatenate(
        [right_tmp[pl.ds(k, rows, stride=4), 0:32] for k in range(4)], axis=1
    )
    fill(left_ref, left)
    y, zl = lax.axis_index("y"), lax.axis_index("zl")
    side = jnp.where(y == zl, lax.rem(y, 2), jnp.where(y < zl, 1, 0))
    for k in range(8):
        right_ref[k] = jnp.where(side == k // 4, right, 0.0)


CHUNK = 8


def outer_kernel(
    left_ref, right_ref, state_ref, spread_ref, small_ref, out_ref, turned
):
    lefts = [left_ref[pl.ds(g, 64, stride=6), :] * (1.0 / 64.0) for g in range(6)]
    lh, ll = split(jnp.concatenate(lefts, axis=1))
    left4 = jnp.concatenate([lh, lh, ll, ll], axis=0)
    for core in range(2):
        for g in range(6):
            block = jnp.concatenate(
                [
                    right_ref[pl.ds((y * 2 + core) * 96 + g, 16, stride=6), :]
                    for y in RING
                ],
                axis=0,
            )
            high = block.astype(BF16).astype(F32)
            stacked = jnp.concatenate([high, block - high], axis=0)
            turned[(core * 6 + g) * LANES : (core * 6 + g + 1) * LANES, :] = stacked.T
    rights = []
    for d in range(32):
        right = turned[pl.ds(d, 48, stride=32), :].astype(BF16)
        rights.append(jnp.concatenate([right, right], axis=1))
    right4 = jnp.concatenate(rights, axis=0)
    lane = lax.broadcasted_iota(jnp.int32, (48, LANES), 1)
    low_half = lane < 64
    even = lax.rem(lax.div(lane, 32), 2) == 0

    def exchange(a, b, shift, keep):
        return (
            jnp.where(keep, a, pltpu.roll(b, shift, 1)),
            jnp.where(keep, pltpu.roll(a, LANES - shift, 1), b),
        )

    for pair in range(6 // 6):
        product = dot(right4, left4[:, pair * 6 * LANES : (pair + 1) * 6 * LANES])
        rows = []
        for g in range(6):
            lanes = slice(g * LANES, (g + 1) * LANES)
            pieces = [[], [], [], []]
            for t in range(0, 32, 4):
                p0, p1, p2, p3 = (
                    product[(t + e) * 48 : (t + e + 1) * 48, lanes] for e in range(4)
                )
                a0, a2 = exchange(p0, p2, 64, low_half)
                a1, a3 = exchange(p1, p3, 64, low_half)
                k0, k1 = exchange(a0, a1, 32, even)
                k2, k3 = exchange(a2, a3, 32, even)
                for k, piece in enumerate((k0, k1, k2, k3)):
                    pieces[k].append(piece)
            rows += [jnp.concatenate(piece, axis=1) for piece in pieces]
        ah, al = split(jnp.concatenate(rows, axis=0))
        update = dot(jnp.concatenate([ah, al], axis=1), spread_ref[...])
        for n in range(4 * 6):
            i = pair * 4 * 6 + n
            part = update[n * 48 : (n + 1) * 48]
            out_ref[i] = (
                state_ref[i] + (part[:, :LANES] + part[:, LANES:]) + small_ref[1:2, :]
            )


def mirrored():
    sides = [((a, b), (b, a)) for a in range(4) for b in range(a + 1, 4)]
    sides += [((a, a), (a + 1, a + 1)) for a in (0, 2)]

    def index(y, zh, core, zl, x):
        return (((y * 4 + zh) * 2 + core) * 4 + zl) * 4 + x

    return [
        [index(y, zh, core, zl, x) for y, zl in pair for zh in FAR]
        for core in range(2)
        for x in range(4)
        for pair in sides
    ]


PREPARE = pltpu.CompilerParams(vmem_limit_bytes=62 * 1024 * 1024)
PARAMS = pltpu.CompilerParams(vmem_limit_bytes=48 * 1024 * 1024)


OUTER_SCRATCH = [pltpu.VMEM((1536, 128), F32)]


def shape(*dims):
    return jax.ShapeDtypeStruct(dims, F32)


def on_device(
    alignment,
    pair_state,
    pair_weights,
    align_gain,
    value_weight,
    gate_weight,
    output_weight,
    outer_gain,
    left_weight,
    right_weight,
    outer_weight,
    outer_bias,
):
    align_gain, outer_gain = align_gain[None], outer_gain[None]
    normed = pl.pallas_call(
        features_kernel, out_shape=shape(4, 48, 128), compiler_params=PREPARE
    )(alignment, align_gain)
    packed, gate, spread, small = pl.pallas_call(
        early_kernel,
        out_shape=(
            shape(16, 72, 128),
            shape(24, 1024),
            jax.ShapeDtypeStruct((2048, 256), BF16),
            shape(8, 128),
        ),
        compiler_params=PARAMS,
    )(
        pair_weights,
        alignment,
        gate_weight,
        outer_weight,
        align_gain,
        outer_gain,
        outer_bias[None],
    )
    near = lax.all_to_all(
        normed, "zh", 0, 0, axis_index_groups=[list(FAR)], tiled=True
    ).reshape(192, 128)
    near, packed = lax.optimization_barrier((near, packed))
    weights = lax.all_to_all(packed, COL, 0, 0, axis_index_groups=[list(MIDDLE)], tiled=True)
    gathered = lax.all_gather(near, ("y", "core"), axis=0, tiled=True).reshape(32, 48, 128)
    alignment_out, left, right = pl.pallas_call(
        average_kernel,
        out_shape=(shape(24, 4, 64), shape(24, 128), shape(8, 24, 128)),
        scratch_shapes=[pltpu.VMEM((96, 128), F32), pltpu.VMEM((96, 128), F32)],
        compiler_params=PARAMS,
    )(
        weights,
        gathered,
        gate,
        small,
        alignment,
        value_weight,
        output_weight.T,
        left_weight.T,
        right_weight.T,
    )
    right = lax.all_to_all(right, ALL, 0, 0, axis_index_groups=mirrored(), tiled=True)
    left = lax.all_gather(left, "x", axis=0, tiled=True)
    right, left = lax.optimization_barrier((right, left))
    right = pl.pallas_call(
        copies_kernel, out_shape=shape(32, 24, 128), compiler_params=PARAMS
    )(right)
    right_all = lax.all_to_all(right, ("y", "core", "x"), 0, 0, tiled=True)
    right_all = right_all.reshape(768, 128)
    left_all = lax.all_gather(left, "zl", axis=0, axis_index_groups=[list(RING)], tiled=True)
    pair_out = pl.pallas_call(
        outer_kernel,
        out_shape=shape(24, 48, 128),
        scratch_shapes=OUTER_SCRATCH,
        compiler_params=PARAMS,
    )(left_all, right_all, pair_state, spread, small)
    return alignment_out, pair_out


def solution(mesh):
    torus = Mesh(mesh.devices.reshape(4, 4, 2, 4, 4), ALL)
    return jax.shard_map(
        on_device,
        mesh=torus,
        in_specs=(P(ROW, COL, None), P(ROW, COL, None), P(None, ROW, COL)) + (P(),) * 9,
        out_specs=(P(ROW, COL, None), P(ROW, COL, None)),
        check_vma=False,
    )
```

```python
import functools

import jax
import jax.numpy as jnp
from jax import lax
from jax.experimental import pallas as pl
from jax.experimental.pallas import tpu as pltpu
from jax.sharding import Mesh, PartitionSpec as P

F32 = jnp.float32
BF16 = jnp.bfloat16
ROW = ("y", "zh", "core")
COL = ("zl", "x")
ALL = ROW + COL
FAR = (2, 0, 3, 1)
RING = (0, 2, 3, 1)
MIDDLE = (6, *range(6), *range(7, 16))
LANES = 128
HALVES = (slice(0, 64), slice(64, 128))


def split(value):
    high = value.astype(BF16)
    low = (value - high.astype(F32)).astype(BF16)
    return high, low


def dot(a, b):
    return jnp.dot(a, b, preferred_element_type=F32)


def dot3(a, b):
    ah, al = split(a)
    bh, bl = split(b)
    return dot(ah, bh) + (dot(ah, bl) + dot(al, bh))


def normalize(features, gain):
    mean = jnp.mean(features, axis=-1, keepdims=True)
    centered = features - mean
    spread = jnp.mean(centered * centered, axis=-1, keepdims=True)
    return centered * lax.rsqrt(spread + 1e-05) * gain


def twice(weight):
    zeros = jnp.zeros_like(weight)
    return jnp.concatenate(
        [jnp.concatenate([weight, zeros], 1), jnp.concatenate([zeros, weight], 1)], 0
    )


def fill(ref, value):
    if len(ref.shape) == 2:
        ref[...] = value
    else:
        for k in range(ref.shape[0]):
            ref[k] = value


def features_kernel(align_ref, gain_ref, normed_ref):
    parts = [normalize(align_ref[:, s, :], gain_ref[...]) for s in range(4)]
    features = jnp.concatenate(
        [jnp.concatenate(parts[0:2], axis=1), jnp.concatenate(parts[2:4], axis=1)], axis=0
    )
    fill(normed_ref, features)


def early_kernel(
    pair_w_ref,
    align_ref,
    gate_w_ref,
    outer_ref,
    align_gain_ref,
    outer_gain_ref,
    bias_ref,
    weights_ref,
    gate_ref,
    spread_ref,
    small_ref,
):
    heads, rows, columns = pair_w_ref.shape
    turned = pair_w_ref[...].reshape(heads * rows, columns).T
    half = columns // 2
    tail = turned[:, LANES:]
    tail = jnp.concatenate([tail[:half], tail[half:]], axis=1)
    fill(weights_ref, jnp.concatenate([turned[:, :LANES], tail], axis=0))
    small_ref[0:1, 0:64] = outer_gain_ref[...]
    small_ref[1:2, :] = bias_ref[...]
    own = [normalize(align_ref[:, s, :], align_gain_ref[...]) for s in range(4)]
    logits = dot3(jnp.concatenate(own, axis=0), gate_w_ref[...])
    for s in range(4):
        gate_ref[:, s * 256 : (s + 1) * 256] = jax.nn.sigmoid(logits[s * rows : (s + 1) * rows])
    for d in range(32):
        wh, wl = split(outer_ref[pl.ds(d, 32, stride=32), :])
        both = jnp.concatenate([wh, wl], axis=1)
        spread_ref[pl.ds(d * 32, 32), :] = both
        spread_ref[pl.ds(1024 + d * 32, 32), :] = both


def copies_kernel(blocks_ref, out_ref):
    for x in range(4):
        at = FAR.index(x)
        block = blocks_ref[at] + blocks_ref[at + 4]
        for k in range(8):
            out_ref[4 * k + x] = block


def dot3_turned(a, b):
    ah, al = split(a)
    bh, bl = split(b)

    def one(x, y):
        return lax.dot_general(x, y, (((1,), (1,)), ((), ())), preferred_element_type=F32)

    return one(ah, bh) + (one(ah, bl) + one(al, bh))


def turned_dot(a, b):
    return lax.dot_general(a, b, (((0,), (0,)), ((), ())), preferred_element_type=F32)


def landed(row):
    y, zh, core = row // 8, row // 2 % 4, row % 2
    return (y * 2 + core) * 4 + FAR.index(zh)


def average_kernel(
    weights_ref,
    gathered_ref,
    gate_ref,
    small_ref,
    align_ref,
    value_ref,
    output_ref,
    left_w_ref,
    right_w_ref,
    out_ref,
    left_ref,
    right_ref,
    left_tmp,
):
    rows = align_ref.shape[0]
    columns = 2 * rows
    heads = 8
    order = [MIDDLE.index(c) for c in range(16)]
    first = jnp.concatenate([weights_ref[k, 0:columns, :] for k in order], axis=0)
    tails = [weights_ref[k, columns:, :] for k in order]
    second = jnp.concatenate([t[:, half] for t in tails for half in HALVES], axis=0)
    weights = jnp.concatenate([first, second], axis=1)
    wh, wl = split(weights)
    mixed = []
    for p in range(2):
        blocks = [
            gathered_ref[landed(r), p * rows : (p + 1) * rows, :] for r in range(32)
        ]
        fh, fl = split(jnp.concatenate(blocks, axis=0))
        mixed.append(turned_dot(wh, fh) + (turned_dot(wh, fl) + turned_dot(wl, fh)))
    lane = lax.broadcasted_iota(jnp.int32, (rows, 512), 1)
    lane_head = lax.rem(lax.div(lane, 32), heads)
    vh, vl = split(twice(value_ref[...]))
    gated = []
    for p in range(2):
        mh, ml = split(mixed[p])
        by_head = dot(mh, vh) + (dot(mh, vl) + dot(ml, vh))
        averaged = jnp.zeros((rows, 512), F32)
        for h in range(heads):
            averaged += jnp.where(lane_head == h, by_head[h * rows : (h + 1) * rows], 0.0)
        product = gate_ref[:, p * 512 : (p + 1) * 512] * averaged
        gated += [product[:, :256], product[:, 256:]]
    update = dot3_turned(jnp.concatenate(gated, axis=0), output_ref[...])
    aligned = jnp.concatenate([align_ref[:, s, :] for s in range(4)], axis=0) + update
    for s in range(4):
        out_ref[:, s, :] = aligned[s * rows : (s + 1) * rows]
    normed = normalize(aligned, small_ref[0:1, 0:64])
    both = jnp.concatenate([left_w_ref[...], right_w_ref[...]], axis=0)
    left_tmp[:, 0:64] = dot3_turned(normed, both)
    left = jnp.concatenate(
        [left_tmp[pl.ds(k, rows, stride=4), 0:32] for k in range(4)], axis=1
    )
    right = jnp.concatenate(
        [left_tmp[pl.ds(k, rows, stride=4), :][:, 32:64] for k in range(4)], axis=1
    )
    fill(left_ref, left)
    y, zl = lax.axis_index("y"), lax.axis_index("zl")
    side = jnp.where(y == zl, lax.rem(y, 2), jnp.where(y < zl, 1, 0))
    for k in range(8):
        right_ref[k] = jnp.where(side == k // 4, right, 0.0)


CHUNK = 8


def outer_kernel(
    left_ref, right_ref, state_ref, spread_ref, small_ref, out_ref, turned
):
    lefts = [left_ref[pl.ds(g, 64, stride=6), :] * (1.0 / 64.0) for g in range(6)]
    lh, ll = split(jnp.concatenate(lefts, axis=1))
    left4 = jnp.concatenate([lh, lh, ll, ll], axis=0)
    for core in range(2):
        for g in range(6):
            block = jnp.concatenate(
                [
                    right_ref[pl.ds((y * 2 + core) * 96 + g, 16, stride=6), :]
                    for y in RING
                ],
                axis=0,
            )
            high = block.astype(BF16).astype(F32)
            stacked = jnp.concatenate([high, block - high], axis=0)
            turned[(core * 6 + g) * LANES : (core * 6 + g + 1) * LANES, :] = stacked.T
    rights = []
    for d in range(32):
        right = turned[pl.ds(d, 48, stride=32), :].astype(BF16)
        rights.append(jnp.concatenate([right, right], axis=1))
    right4 = jnp.concatenate(rights, axis=0)
    lane = lax.broadcasted_iota(jnp.int32, (48, LANES), 1)
    low_half = lane < 64
    even = lax.rem(lax.div(lane, 32), 2) == 0

    def exchange(a, b, shift, keep):
        return (
            jnp.where(keep, a, pltpu.roll(b, shift, 1)),
            jnp.where(keep, pltpu.roll(a, LANES - shift, 1), b),
        )

    for pair in range(6 // 6):
        product = dot(right4, left4[:, pair * 6 * LANES : (pair + 1) * 6 * LANES])
        rows = []
        for g in range(6):
            lanes = slice(g * LANES, (g + 1) * LANES)
            pieces = [[], [], [], []]
            for t in range(0, 32, 4):
                p0, p1, p2, p3 = (
                    product[(t + e) * 48 : (t + e + 1) * 48, lanes] for e in range(4)
                )
                a0, a2 = exchange(p0, p2, 64, low_half)
                a1, a3 = exchange(p1, p3, 64, low_half)
                k0, k1 = exchange(a0, a1, 32, even)
                k2, k3 = exchange(a2, a3, 32, even)
                for k, piece in enumerate((k0, k1, k2, k3)):
                    pieces[k].append(piece)
            rows += [jnp.concatenate(piece, axis=1) for piece in pieces]
        ah, al = split(jnp.concatenate(rows, axis=0))
        update = dot(jnp.concatenate([ah, al], axis=1), spread_ref[...])
        for n in range(4 * 6):
            i = pair * 4 * 6 + n
            part = update[n * 48 : (n + 1) * 48]
            out_ref[i] = (
                state_ref[i] + (part[:, :LANES] + part[:, LANES:]) + small_ref[1:2, :]
            )


def mirrored():
    sides = [((a, b), (b, a)) for a in range(4) for b in range(a + 1, 4)]
    sides += [((a, a), (a + 1, a + 1)) for a in (0, 2)]

    def index(y, zh, core, zl, x):
        return (((y * 4 + zh) * 2 + core) * 4 + zl) * 4 + x

    return [
        [index(y, zh, core, zl, x) for y, zl in pair for zh in FAR]
        for core in range(2)
        for x in range(4)
        for pair in sides
    ]


PREPARE = pltpu.CompilerParams(vmem_limit_bytes=62 * 1024 * 1024)
PARAMS = pltpu.CompilerParams(vmem_limit_bytes=48 * 1024 * 1024)


OUTER_SCRATCH = [pltpu.VMEM((1536, 128), F32)]


def shape(*dims):
    return jax.ShapeDtypeStruct(dims, F32)


def on_device(
    alignment,
    pair_state,
    pair_weights,
    align_gain,
    value_weight,
    gate_weight,
    output_weight,
    outer_gain,
    left_weight,
    right_weight,
    outer_weight,
    outer_bias,
):
    align_gain, outer_gain = align_gain[None], outer_gain[None]
    normed = pl.pallas_call(
        features_kernel, out_shape=shape(4, 48, 128), compiler_params=PREPARE
    )(alignment, align_gain)
    packed, gate, spread, small = pl.pallas_call(
        early_kernel,
        out_shape=(
            shape(16, 72, 128),
            shape(24, 1024),
            jax.ShapeDtypeStruct((2048, 256), BF16),
            shape(8, 128),
        ),
        compiler_params=PARAMS,
    )(
        pair_weights,
        alignment,
        gate_weight,
        outer_weight,
        align_gain,
        outer_gain,
        outer_bias[None],
    )
    near = lax.all_to_all(
        normed, "zh", 0, 0, axis_index_groups=[list(FAR)], tiled=True
    ).reshape(192, 128)
    near, packed = lax.optimization_barrier((near, packed))
    weights = lax.all_to_all(packed, COL, 0, 0, axis_index_groups=[list(MIDDLE)], tiled=True)
    gathered = lax.all_gather(near, ("y", "core"), axis=0, tiled=True).reshape(32, 48, 128)
    alignment_out, left, right = pl.pallas_call(
        average_kernel,
        out_shape=(shape(24, 4, 64), shape(24, 128), shape(8, 24, 128)),
        scratch_shapes=[pltpu.VMEM((96, 128), F32)],
        compiler_params=PARAMS,
    )(
        weights,
        gathered,
        gate,
        small,
        alignment,
        value_weight,
        output_weight.T,
        left_weight.T,
        right_weight.T,
    )
    right = lax.all_to_all(right, ALL, 0, 0, axis_index_groups=mirrored(), tiled=True)
    left = lax.all_gather(left, "x", axis=0, tiled=True)
    right, left = lax.optimization_barrier((right, left))
    right = pl.pallas_call(
        copies_kernel, out_shape=shape(32, 24, 128), compiler_params=PARAMS
    )(right)
    right_all = lax.all_to_all(right, ("y", "core", "x"), 0, 0, tiled=True)
    right_all = right_all.reshape(768, 128)
    left_all = lax.all_gather(left, "zl", axis=0, axis_index_groups=[list(RING)], tiled=True)
    pair_out = pl.pallas_call(
        outer_kernel,
        out_shape=shape(24, 48, 128),
        scratch_shapes=OUTER_SCRATCH,
        compiler_params=PARAMS,
    )(left_all, right_all, pair_state, spread, small)
    return alignment_out, pair_out


def solution(mesh):
    torus = Mesh(mesh.devices.reshape(4, 4, 2, 4, 4), ALL)
    return jax.shard_map(
        on_device,
        mesh=torus,
        in_specs=(P(ROW, COL, None), P(ROW, COL, None), P(None, ROW, COL)) + (P(),) * 9,
        out_specs=(P(ROW, COL, None), P(ROW, COL, None)),
        check_vma=False,
    )
```

```python
import functools

import jax
import jax.numpy as jnp
from jax import lax
from jax.experimental import pallas as pl
from jax.experimental.pallas import tpu as pltpu
from jax.sharding import Mesh, PartitionSpec as P

F32 = jnp.float32
BF16 = jnp.bfloat16
ROW = ("y", "zh", "core")
COL = ("zl", "x")
ALL = ROW + COL
FAR = (2, 3, 1, 0)
RING = (0, 2, 3, 1)
MIDDLE = (6, *range(6), *range(7, 16))
LANES = 128
HALVES = (slice(0, 64), slice(64, 128))


def split(value):
    high = value.astype(BF16)
    low = (value - high.astype(F32)).astype(BF16)
    return high, low


def dot(a, b):
    return jnp.dot(a, b, preferred_element_type=F32)


def dot3(a, b):
    ah, al = split(a)
    bh, bl = split(b)
    return dot(ah, bh) + (dot(ah, bl) + dot(al, bh))


def normalize(features, gain):
    mean = jnp.mean(features, axis=-1, keepdims=True)
    centered = features - mean
    spread = jnp.mean(centered * centered, axis=-1, keepdims=True)
    return centered * lax.rsqrt(spread + 1e-05) * gain


def twice(weight):
    zeros = jnp.zeros_like(weight)
    return jnp.concatenate(
        [jnp.concatenate([weight, zeros], 1), jnp.concatenate([zeros, weight], 1)], 0
    )


def fill(ref, value):
    if len(ref.shape) == 2:
        ref[...] = value
    else:
        for k in range(ref.shape[0]):
            ref[k] = value


def features_kernel(align_ref, gain_ref, normed_ref):
    parts = [normalize(align_ref[:, s, :], gain_ref[...]) for s in range(4)]
    features = jnp.concatenate(
        [jnp.concatenate(parts[0:2], axis=1), jnp.concatenate(parts[2:4], axis=1)], axis=0
    )
    fill(normed_ref, features)


def early_kernel(
    pair_w_ref,
    align_ref,
    gate_w_ref,
    outer_ref,
    align_gain_ref,
    outer_gain_ref,
    bias_ref,
    weights_ref,
    gate_ref,
    spread_ref,
    small_ref,
):
    heads, rows, columns = pair_w_ref.shape
    turned = pair_w_ref[...].reshape(heads * rows, columns).T
    half = columns // 2
    tail = turned[:, LANES:]
    tail = jnp.concatenate([tail[:half], tail[half:]], axis=1)
    fill(weights_ref, jnp.concatenate([turned[:, :LANES], tail], axis=0))
    small_ref[0:1, 0:64] = outer_gain_ref[...]
    small_ref[1:2, :] = bias_ref[...]
    own = [normalize(align_ref[:, s, :], align_gain_ref[...]) for s in range(4)]
    logits = dot3(jnp.concatenate(own, axis=0), gate_w_ref[...])
    for s in range(4):
        gate_ref[:, s * 256 : (s + 1) * 256] = jax.nn.sigmoid(logits[s * rows : (s + 1) * rows])
    for d in range(32):
        wh, wl = split(outer_ref[pl.ds(d, 32, stride=32), :])
        both = jnp.concatenate([wh, wl], axis=1)
        spread_ref[pl.ds(d * 32, 32), :] = both
        spread_ref[pl.ds(1024 + d * 32, 32), :] = both


def copies_kernel(blocks_ref, out_ref):
    for x in range(4):
        at = FAR.index(x)
        block = blocks_ref[at] + blocks_ref[at + 4]
        for k in range(8):
            out_ref[4 * k + x] = block


def dot3_turned(a, b):
    ah, al = split(a)
    bh, bl = split(b)

    def one(x, y):
        return lax.dot_general(x, y, (((1,), (1,)), ((), ())), preferred_element_type=F32)

    return one(ah, bh) + (one(ah, bl) + one(al, bh))


def turned_dot(a, b):
    return lax.dot_general(a, b, (((0,), (0,)), ((), ())), preferred_element_type=F32)


def landed(row):
    y, zh, core = row // 8, row // 2 % 4, row % 2
    return (y * 2 + core) * 4 + FAR.index(zh)


def average_kernel(
    weights_ref,
    gathered_ref,
    gate_ref,
    small_ref,
    align_ref,
    value_ref,
    output_ref,
    left_w_ref,
    right_w_ref,
    out_ref,
    left_ref,
    right_ref,
    left_tmp,
):
    rows = align_ref.shape[0]
    columns = 2 * rows
    heads = 8
    order = [MIDDLE.index(c) for c in range(16)]
    first = jnp.concatenate([weights_ref[k, 0:columns, :] for k in order], axis=0)
    tails = [weights_ref[k, columns:, :] for k in order]
    second = jnp.concatenate([t[:, half] for t in tails for half in HALVES], axis=0)
    weights = jnp.concatenate([first, second], axis=1)
    wh, wl = split(weights)
    mixed = []
    for p in range(2):
        blocks = [
            gathered_ref[landed(r), p * rows : (p + 1) * rows, :] for r in range(32)
        ]
        fh, fl = split(jnp.concatenate(blocks, axis=0))
        mixed.append(turned_dot(wh, fh) + (turned_dot(wh, fl) + turned_dot(wl, fh)))
    lane = lax.broadcasted_iota(jnp.int32, (rows, 512), 1)
    lane_head = lax.rem(lax.div(lane, 32), heads)
    vh, vl = split(twice(value_ref[...]))
    gated = []
    for p in range(2):
        mh, ml = split(mixed[p])
        by_head = dot(mh, vh) + (dot(mh, vl) + dot(ml, vh))
        averaged = jnp.zeros((rows, 512), F32)
        for h in range(heads):
            averaged += jnp.where(lane_head == h, by_head[h * rows : (h + 1) * rows], 0.0)
        product = gate_ref[:, p * 512 : (p + 1) * 512] * averaged
        gated += [product[:, :256], product[:, 256:]]
    update = dot3_turned(jnp.concatenate(gated, axis=0), output_ref[...])
    aligned = jnp.concatenate([align_ref[:, s, :] for s in range(4)], axis=0) + update
    for s in range(4):
        out_ref[:, s, :] = aligned[s * rows : (s + 1) * rows]
    normed = normalize(aligned, small_ref[0:1, 0:64])
    both = jnp.concatenate([left_w_ref[...], right_w_ref[...]], axis=0)
    left_tmp[:, 0:64] = dot3_turned(normed, both)
    left = jnp.concatenate(
        [left_tmp[pl.ds(k, rows, stride=4), 0:32] for k in range(4)], axis=1
    )
    right = jnp.concatenate(
        [left_tmp[pl.ds(k, rows, stride=4), :][:, 32:64] for k in range(4)], axis=1
    )
    fill(left_ref, left)
    y, zl = lax.axis_index("y"), lax.axis_index("zl")
    side = jnp.where(y == zl, lax.rem(y, 2), jnp.where(y < zl, 1, 0))
    for k in range(8):
        right_ref[k] = jnp.where(side == k // 4, right, 0.0)


CHUNK = 8


def outer_kernel(
    left_ref, right_ref, state_ref, spread_ref, small_ref, out_ref, turned
):
    lefts = [left_ref[pl.ds(g, 64, stride=6), :] * (1.0 / 64.0) for g in range(6)]
    lh, ll = split(jnp.concatenate(lefts, axis=1))
    left4 = jnp.concatenate([lh, lh, ll, ll], axis=0)
    for core in range(2):
        for g in range(6):
            block = jnp.concatenate(
                [
                    right_ref[pl.ds((y * 2 + core) * 96 + g, 16, stride=6), :]
                    for y in RING
                ],
                axis=0,
            )
            high = block.astype(BF16).astype(F32)
            stacked = jnp.concatenate([high, block - high], axis=0)
            turned[(core * 6 + g) * LANES : (core * 6 + g + 1) * LANES, :] = stacked.T
    rights = []
    for d in range(32):
        right = turned[pl.ds(d, 48, stride=32), :].astype(BF16)
        rights.append(jnp.concatenate([right, right], axis=1))
    right4 = jnp.concatenate(rights, axis=0)
    lane = lax.broadcasted_iota(jnp.int32, (48, LANES), 1)
    low_half = lane < 64
    even = lax.rem(lax.div(lane, 32), 2) == 0

    def exchange(a, b, shift, keep):
        return (
            jnp.where(keep, a, pltpu.roll(b, shift, 1)),
            jnp.where(keep, pltpu.roll(a, LANES - shift, 1), b),
        )

    for pair in range(6 // 6):
        product = dot(right4, left4[:, pair * 6 * LANES : (pair + 1) * 6 * LANES])
        rows = []
        for g in range(6):
            lanes = slice(g * LANES, (g + 1) * LANES)
            pieces = [[], [], [], []]
            for t in range(0, 32, 4):
                p0, p1, p2, p3 = (
                    product[(t + e) * 48 : (t + e + 1) * 48, lanes] for e in range(4)
                )
                a0, a2 = exchange(p0, p2, 64, low_half)
                a1, a3 = exchange(p1, p3, 64, low_half)
                k0, k1 = exchange(a0, a1, 32, even)
                k2, k3 = exchange(a2, a3, 32, even)
                for k, piece in enumerate((k0, k1, k2, k3)):
                    pieces[k].append(piece)
            rows += [jnp.concatenate(piece, axis=1) for piece in pieces]
        ah, al = split(jnp.concatenate(rows, axis=0))
        update = dot(jnp.concatenate([ah, al], axis=1), spread_ref[...])
        for n in range(4 * 6):
            i = pair * 4 * 6 + n
            part = update[n * 48 : (n + 1) * 48]
            out_ref[i] = (
                state_ref[i] + (part[:, :LANES] + part[:, LANES:]) + small_ref[1:2, :]
            )


def mirrored():
    sides = [((a, b), (b, a)) for a in range(4) for b in range(a + 1, 4)]
    sides += [((a, a), (a + 1, a + 1)) for a in (0, 2)]

    def index(y, zh, core, zl, x):
        return (((y * 4 + zh) * 2 + core) * 4 + zl) * 4 + x

    return [
        [index(y, zh, core, zl, x) for y, zl in pair for zh in FAR]
        for core in range(2)
        for x in range(4)
        for pair in sides
    ]


PREPARE = pltpu.CompilerParams(vmem_limit_bytes=62 * 1024 * 1024)
PARAMS = pltpu.CompilerParams(vmem_limit_bytes=48 * 1024 * 1024)


OUTER_SCRATCH = [pltpu.VMEM((1536, 128), F32)]


def shape(*dims):
    return jax.ShapeDtypeStruct(dims, F32)


def on_device(
    alignment,
    pair_state,
    pair_weights,
    align_gain,
    value_weight,
    gate_weight,
    output_weight,
    outer_gain,
    left_weight,
    right_weight,
    outer_weight,
    outer_bias,
):
    align_gain, outer_gain = align_gain[None], outer_gain[None]
    normed = pl.pallas_call(
        features_kernel, out_shape=shape(4, 48, 128), compiler_params=PREPARE
    )(alignment, align_gain)
    packed, gate, spread, small = pl.pallas_call(
        early_kernel,
        out_shape=(
            shape(16, 72, 128),
            shape(24, 1024),
            jax.ShapeDtypeStruct((2048, 256), BF16),
            shape(8, 128),
        ),
        compiler_params=PARAMS,
    )(
        pair_weights,
        alignment,
        gate_weight,
        outer_weight,
        align_gain,
        outer_gain,
        outer_bias[None],
    )
    near = lax.all_to_all(
        normed, "zh", 0, 0, axis_index_groups=[list(FAR)], tiled=True
    ).reshape(192, 128)
    near, packed = lax.optimization_barrier((near, packed))
    weights = lax.all_to_all(packed, COL, 0, 0, axis_index_groups=[list(MIDDLE)], tiled=True)
    gathered = lax.all_gather(near, ("y", "core"), axis=0, tiled=True).reshape(32, 48, 128)
    alignment_out, left, right = pl.pallas_call(
        average_kernel,
        out_shape=(shape(24, 4, 64), shape(24, 128), shape(8, 24, 128)),
        scratch_shapes=[pltpu.VMEM((96, 128), F32)],
        compiler_params=PARAMS,
    )(
        weights,
        gathered,
        gate,
        small,
        alignment,
        value_weight,
        output_weight.T,
        left_weight.T,
        right_weight.T,
    )
    right = lax.all_to_all(right, ALL, 0, 0, axis_index_groups=mirrored(), tiled=True)
    left = lax.all_gather(left, "x", axis=0, tiled=True)
    right, left = lax.optimization_barrier((right, left))
    right = pl.pallas_call(
        copies_kernel, out_shape=shape(32, 24, 128), compiler_params=PARAMS
    )(right)
    right_all = lax.all_to_all(right, ("y", "core", "x"), 0, 0, tiled=True)
    right_all = right_all.reshape(768, 128)
    left_all = lax.all_gather(left, "zl", axis=0, axis_index_groups=[list(RING)], tiled=True)
    pair_out = pl.pallas_call(
        outer_kernel,
        out_shape=shape(24, 48, 128),
        scratch_shapes=OUTER_SCRATCH,
        compiler_params=PARAMS,
    )(left_all, right_all, pair_state, spread, small)
    return alignment_out, pair_out


def solution(mesh):
    torus = Mesh(mesh.devices.reshape(4, 4, 2, 4, 4), ALL)
    return jax.shard_map(
        on_device,
        mesh=torus,
        in_specs=(P(ROW, COL, None), P(ROW, COL, None), P(None, ROW, COL)) + (P(),) * 9,
        out_specs=(P(ROW, COL, None), P(ROW, COL, None)),
        check_vma=False,
    )
```
